128 devices in a mesh: tm: 16 (over z, y), rows: 8 (over x, core).
Axes of the slice: x: 4, y: 4, z: 4, core: 2. Of those that a mesh axis runs over, the one named last changes fastest.
Arguments:
- features: bfloat16 [64, 32, 64, 128], P('tm', 'rows'), may hold values from -6 to 6
- cotangent: bfloat16 [64, 32, 64, 128], P('tm', 'rows'), may hold values from -6 to 6
- first_kernel: bfloat16 [3, 3, 3, 128, 128], replicated, may hold values from -0.109375 to 0.109375
- second_kernel: bfloat16 [3, 3, 3, 128, 128], replicated, may hold values from -0.109375 to 0.109375
Outputs:
- block_out: bfloat16 [64, 32, 64, 128], P('tm', 'rows')
- grad_input: bfloat16 [64, 32, 64, 128], P('tm', 'rows')
- grad_first: float32 [3, 3, 3, 128, 128], P(None, None, None, None, 'tm')
- grad_second: float32 [3, 3, 3, 128, 128], P(None, None, None, None, 'tm')
The draws below stay inside these ranges and needn't reach their ends.
All inputs are finite; a program needn't handle non-finite values.
Results may differ from the reference program's by a relative error of at most 0.0053.
Values may be sent and summed in bfloat16 or wider, within the bound.
A program may use at most 128 MiB of HBM per device.

```python
import jax
import jax.numpy as jnp
from jax import lax

C = 128
WIDTH = 64
FRAMES = 64
HEIGHT = 32


def level_of(own_key, shape, pieces, low, high):
    factor_of = 1.0
    for axis_at, blocks in pieces:
        heights = jax.random.uniform(jax.random.fold_in(jax.random.fold_in(own_key, 6), axis_at), (blocks,), jnp.float32, low / len(pieces), high / len(pieces))
        factor_of = factor_of * jnp.repeat(jnp.exp(heights), shape[axis_at] // blocks).reshape((-1,) + (1,) * (len(shape) - 1 - axis_at))
    return factor_of


def scatter_about(key, shape, scale, reach, split=(), kind=jnp.bfloat16):
    result = jax.random.normal(key, shape, jnp.float32) * scale
    if len(split) > 0:
        result = level_of(key, shape, split, -0.22, 0.18) * result
    return jnp.clip(result, min=-reach, max=reach).astype(kind)


def setup_inputs(seed: int = 0) -> dict:
    arg_keys = jax.random.split(jax.random.key(seed), 5)
    features = scatter_about(arg_keys[0], (FRAMES, HEIGHT, WIDTH, C), 1.0, 6.0, ((0, 16), (1, 8)))
    cotangent = scatter_about(arg_keys[1], (FRAMES, HEIGHT, WIDTH, C), 1.0, 6.0, ((0, 16), (1, 8)))
    first_kernel = scatter_about(arg_keys[2], (3, 3, 3, C, C), (27 * C) ** -0.5, 0.109375)
    second_kernel = scatter_about(arg_keys[3], (3, 3, 3, C, C), (27 * C) ** -0.5, 0.109375)
    return {"features": features, "cotangent": cotangent, "first_kernel": first_kernel, "second_kernel": second_kernel}


def convolve(field, kernel):
    return lax.conv_general_dilated(field[None], kernel, (1, 1, 1), [(2, 0), (1, 1), (1, 1)], dimension_numbers=('NDHWC', 'DHWIO', 'NDHWC'), precision=lax.Precision.HIGHEST)[0]

def silu_slope(values):
    sigma = jax.nn.sigmoid(values)
    return sigma * (1.0 + values * (1.0 - sigma))

def reference(features, cotangent, first_kernel, second_kernel):
    feats = features.astype(jnp.float32)
    inputs = jax.nn.silu(feats).astype(jnp.bfloat16)
    kernel_one = first_kernel.astype(jnp.float32)
    kernel_two = second_kernel.astype(jnp.float32)
    first_out = convolve(inputs.astype(jnp.float32), kernel_one)
    hidden = jax.nn.silu(first_out).astype(jnp.bfloat16)
    second_out = convolve(hidden.astype(jnp.float32), kernel_two)
    block_out = (feats + second_out).astype(jnp.bfloat16)
    unused, back_two = jax.vjp(convolve, hidden.astype(jnp.float32), kernel_two)
    hidden_grad, second_raw = back_two(cotangent.astype(jnp.float32))
    first_grad = (hidden_grad * silu_slope(first_out)).astype(jnp.bfloat16)
    unused, back_one = jax.vjp(convolve, inputs.astype(jnp.float32), kernel_one)
    input_grad, first_raw = back_one(first_grad.astype(jnp.float32))
    grad_input = (cotangent.astype(jnp.float32) + input_grad * silu_slope(feats)).astype(jnp.bfloat16)
    factor = 1.0 / jnp.sqrt(jnp.float32(FRAMES * HEIGHT * WIDTH))
    return (block_out, grad_input, first_raw * factor, second_raw * factor)
```

```python
import functools
import math

import jax
import jax.numpy as jnp
from jax import lax
from jax.experimental import pallas as pl
from jax.experimental.pallas import tpu as pltpu
from jax.sharding import PartitionSpec as P

C = 128
MESH = pl.DeviceIdType.MESH
F32 = jnp.float32
BF16 = jnp.bfloat16


def zero_shift(values, step, width):
    if step == 0:
        return values
    rows = values.shape[0]
    column = lax.broadcasted_iota(jnp.int32, values.shape, 0) % width
    rolled = pltpu.roll(values, (-step) % rows, 0)
    edge = width - 1 if step > 0 else 0
    return jnp.where(column == edge, 0.0, rolled)


def kernel(
    geom, feat, cot, k1, k2, out_b, out_g, out_1, out_2,
    F, X, C_, H, G, W1, V2, W2, V1, slope, LT, PP, R0, S1, R1, S2, R2, S3, R3, D, ob, og, o1, o2,
    wsem, lsem, hsend, hrecv, s0, r0, s1, r1, s2, r2, s3, r3, s4, r4,
):
    nz, ny, nx, width, cells_all = geom
    ntm, nrows = nz * ny, nx * 2
    oc = C // ntm
    FR, RT = feat.shape[0], feat.shape[1]
    pairs = RT // 2
    cells = FR * RT * width
    tm, rows = lax.axis_index("tm"), lax.axis_index("rows")
    z, y = tm // ny, tm % ny
    x, core = rows // 2, rows % 2
    nf, ns = ny, nz
    first = (1 - core) * y + core * z
    second = (1 - core) * z + core * y

    def first_peer(d):
        return (1 - core) * (z * ny + (y + d) % ny) + core * (((z + d) % nz) * ny + y)

    def second_peer(d):
        return (1 - core) * (((z + d) % nz) * ny + y) + core * (z * ny + (y + d) % ny)

    def x_peer(d):
        return ((x + d) % nx) * 2 + core

    up, down = (tm + 1) % ntm, (tm + ntm - 1) % ntm
    right, left = (rows + 1) % nrows, (rows + nrows - 1) % nrows
    partner = x * 2 + 1 - core

    loads = {}
    count = [0]

    def load(name, src, dst):
        copy = pltpu.make_async_copy(src, dst, wsem.at[count[0]])
        count[0] += 1
        copy.start()
        loads.setdefault(name, []).append(copy)

    def arrived(name):
        for copy in loads[name]:
            copy.wait()

    load("F", feat, F.at[2 : 2 + FR, 1 : 1 + RT])
    load("C", cot, C_.at[0:FR, 1 : 1 + RT])

    def load_forward(name, src, W):
        for k in range(3):
            for o in range(2):
                load(name, src.at[:, :, k], W.at[k, :, o : o + 3, :, o * C : (o + 1) * C])

    def load_backward(name, src, V):
        for k in range(3):
            for o in range(2):
                for j in range(3):
                    at = o + 2 - j
                    load(name, src.at[:, j, k], V.at[k, :, o * C : (o + 1) * C, at * C : (at + 1) * C])

    load_forward("W1", k1, W1)
    load_backward("V2", k2, V2)
    load_forward("W2", k2, W2)
    load_backward("V1", k1, V1)

    peers = [(up, rows), (up, right), (up, left), (down, rows), (down, right), (down, left), (tm, right), (tm, left)]
    peers += [(first_peer(d), rows) for d in range(1, nf)]
    peers += [(second_peer(d), rows) for d in range(1, ns)]
    peers += [(tm, x_peer(d)) for d in range(1, nx)]
    barrier = pltpu.get_barrier_semaphore()
    for peer in peers:
        pl.semaphore_signal(barrier, inc=1, device_id=peer, device_id_type=MESH)
    pl.semaphore_wait(barrier, len(peers))

    def remote(src, dst, send, recv, peer):
        copy = pltpu.make_async_remote_copy(
            src_ref=src, dst_ref=dst, send_sem=send, recv_sem=recv, device_id=peer, device_id_type=MESH
        )
        copy.start()
        return copy

    sent = []

    def send_halo(which, src, at_f, at_r, dst, before):
        own = 2 if before else 0
        edge_src = slice(at_f + FR - 2, at_f + FR) if before else slice(at_f, at_f + 2)
        edge_dst = slice(0, 2) if before else slice(FR, FR + 2)
        ahead = up if before else down
        whole_src, whole_dst = slice(at_f, at_f + FR), slice(own, own + FR)
        last, start = slice(at_r + RT - 1, at_r + RT), slice(at_r, at_r + 1)
        low, high = slice(0, 1), slice(RT + 1, RT + 2)
        inner_src, inner_dst = slice(at_r, at_r + RT), slice(1, 1 + RT)
        plan = [
            (edge_src, inner_src, edge_dst, inner_dst, (ahead, rows)),
            (edge_src, last, edge_dst, low, (ahead, right)),
            (edge_src, start, edge_dst, high, (ahead, left)),
            (whole_src, last, whole_dst, low, (tm, right)),
            (whole_src, start, whole_dst, high, (tm, left)),
        ]
        copies = []
        for n, (sf, sr, df, dr, peer) in enumerate(plan):
            copies.append(remote(src.at[sf, sr], dst.at[df, dr], hsend.at[which, n], hrecv.at[which, n], peer))
        sent.extend(copies)
        return copies

    def receive_halo(copies, dst, before):
        for copy in copies:
            copy.wait_recv()

        @pl.when(tm == (0 if before else ntm - 1))
        def _():
            at = 0 if before else FR
            dst[at : at + 2] = jnp.zeros((2, RT + 2, width, C), BF16)

        @pl.when(rows == 0)
        def _():
            dst[:, 0] = jnp.zeros((FR + 2, width, C), BF16)

        @pl.when(rows == nrows - 1)
        def _():
            dst[:, RT + 1] = jnp.zeros((FR + 2, width, C), BF16)

    halo_f = send_halo(0, feat, 0, 0, F, True)
    halo_c = send_halo(1, cot, 0, 0, C_, False)

    for W in (W1, W2):
        W[:, :, 3, :, 0:C] = jnp.zeros((3, 3, C, C), BF16)
        W[:, :, 0, :, C : 2 * C] = jnp.zeros((3, 3, C, C), BF16)
    for V in (V1, V2):
        V[:, :, 0:C, 3 * C : 4 * C] = jnp.zeros((3, 3, C, C), BF16)
        V[:, :, C : 2 * C, 0:C] = jnp.zeros((3, 3, C, C), BF16)

    def window(field, lead):
        parts = []
        for pair in range(pairs):
            blocks = []
            for i in lead:
                for r in range(4):
                    blocks.append(field[i : i + FR, 2 * pair + r].reshape(FR * width, C))
            parts.append(jnp.concatenate(blocks, axis=1))
        return jnp.concatenate(parts, axis=0)

    def conv_forward(field, W):
        lhs = window(field, (0, 1, 2))
        total = None
        for k in (1, 0, 2):
            got = jnp.dot(lhs, W[k].reshape(12 * C, 2 * C), preferred_element_type=F32)
            got = zero_shift(got, k - 1, width)
            total = got if total is None else total + got
        return total

    def conv_backward(field, V):
        lhs = window(field, (2, 1, 0))
        total = None
        for k in (1, 0, 2):
            rhs = jnp.concatenate([V[k, i] for i in range(3)], axis=1)
            got = lax.dot_general(lhs, rhs, (((1,), (1,)), ((), ())), preferred_element_type=F32)
            got = zero_shift(got, 1 - k, width)
            total = got if total is None else total + got
        return total

    def put(dst, at_f, at_r, values):
        for pair in range(pairs):
            for o in range(2):
                part = values[pair * FR * width : (pair + 1) * FR * width, o * C : (o + 1) * C]
                dst[at_f : at_f + FR, at_r + 2 * pair + o] = part.reshape(FR, width, C).astype(dst.dtype)

    def get(src, at_f, at_r):
        parts = []
        for pair in range(pairs):
            blocks = [src[at_f : at_f + FR, at_r + 2 * pair + o].reshape(FR * width, C) for o in range(2)]
            parts.append(jnp.concatenate(blocks, axis=1))
        return jnp.concatenate(parts, axis=0).astype(F32)

    arrived("F")
    receive_halo(halo_f, F, True)
    for f in range(FR + 2):
        feats = F[f].astype(F32)
        X[f] = (feats * jax.nn.sigmoid(feats)).astype(BF16)
    arrived("W1")
    first_out = conv_forward(X, W1)
    sigma = jax.nn.sigmoid(first_out)
    put(H, 2, 1, first_out * sigma)
    slope[...] = sigma * (1.0 + first_out * (1.0 - sigma))
    halo_h = send_halo(2, H, 2, 1, H, True)

    arrived("C")
    receive_halo(halo_c, C_, False)
    arrived("V2")
    put(G, 0, 1, conv_backward(C_, V2) * slope[...])
    halo_g = send_halo(3, G, 0, 1, G, False)

    eye = (
        lax.broadcasted_iota(jnp.int32, (C, C), 0) == lax.broadcasted_iota(jnp.int32, (C, C), 1)
    ).astype(BF16)
    per_part = 7

    def kernel_gradient(g, own, field):
        grads = own[0:FR, 1 : 1 + RT].reshape(cells, C).astype(F32)
        for k in range(3):
            moved = zero_shift(grads, 1 - k, width).astype(BF16)
            turned = lax.dot_general(eye, moved, (((1,), (1,)), ((), ())), preferred_element_type=F32)
            LT[k * C : (k + 1) * C] = turned.astype(BF16)
        spots = [(i, j) for i in range(3) for j in range(3)]

        def block(i, j):
            return field[i : i + FR, j : j + RT].reshape(cells, C)

        def store(pair, a, b):
            part, slot = pair // per_part, pair % per_part
            both = jnp.concatenate([a.reshape(ntm, oc, C), b.reshape(ntm, oc, C)], axis=1).astype(BF16)
            for zz in range(nz):
                for yy in range(ny):
                    one, two = (yy, zz) if part == 0 else (zz, yy)
                    PP[g, part, one, two, slot] = both[zz * ny + yy]

        for m in range(5):
            group = spots[2 * m : 2 * m + 2]
            rhs = jnp.concatenate([block(i, j) for i, j in group], axis=1)
            got = jnp.dot(LT[...], rhs, preferred_element_type=F32)
            tail = []
            for n in range(len(group)):
                side = got[:, n * C : (n + 1) * C]
                store(2 * m + n, side[0:C], side[C : 2 * C])
                tail.append(side[2 * C : 3 * C])
            if len(tail) == 1:
                tail.append(jnp.zeros((C, C), F32))
            store(9 + m, tail[0], tail[1])

    def swap_start(g):
        return remote(PP.at[g, 1 - core], R0.at[g], s0.at[g], r0.at[g], (tm, partner))

    def swap_finish(g, copy):
        copy.wait_recv()
        S1[g] = (PP[g, core].astype(F32) + R0[g].astype(F32)).astype(BF16)
        copies = [
            remote(S1.at[g, (first + d) % nf], R1.at[g, d - 1], s1.at[g, d - 1], r1.at[g, d - 1], (first_peer(d), rows))
            for d in range(1, nf)
        ]
        sent.extend(copies)
        return copies

    def first_finish(g, copies):
        for copy in copies:
            copy.wait_recv()
        total = S1[g, first].astype(F32)
        for d in range(1, nf):
            total = total + R1[g, d - 1].astype(F32)
        S2[g] = total.astype(BF16)
        more = [
            remote(S2.at[g, (second + d) % ns], R2.at[g, d - 1], s2.at[g, d - 1], r2.at[g, d - 1], (second_peer(d), rows))
            for d in range(1, ns)
        ]
        sent.extend(more)
        return more

    def second_finish(g, copies):
        for copy in copies:
            copy.wait_recv()
        total = S2[g, second].astype(F32)
        for d in range(1, ns):
            total = total + R2[g, d - 1].astype(F32)
        S3[g] = total.astype(BF16)
        more = [
            remote(S3.at[g], R3.at[g, d - 1], s3.at[g, d - 1], r3.at[g, d - 1], (tm, x_peer(d)))
            for d in range(1, nx)
        ]
        sent.extend(more)
        return more

    scale = 1.0 / math.sqrt(cells_all)

    def third_finish(g, copies):
        for copy in copies:
            copy.wait_recv()
        total = S3[g].astype(F32)
        for d in range(1, nx):
            total = total + R3[g, d - 1].astype(F32)
        D[g, core] = total * scale
        copy = remote(D.at[g, core], D.at[g, core], s4.at[g], r4.at[g], (tm, partner))
        sent.append(copy)
        return copy

    kernel_gradient(0, G, X)
    swap_a = swap_start(0)
    receive_halo(halo_h, H, True)
    kernel_gradient(1, C_, H)
    swap_b = swap_start(1)
    sent.extend([swap_a, swap_b])
    one_a = swap_finish(0, swap_a)
    one_b = swap_finish(1, swap_b)

    arrived("W2")
    put(ob, 0, 0, get(F, 2, 1) + conv_forward(H, W2))
    write_b = pltpu.make_async_copy(ob, out_b, lsem.at[0])
    write_b.start()

    two_a = first_finish(0, one_a)
    two_b = first_finish(1, one_b)

    receive_halo(halo_g, G, False)
    arrived("V1")
    feats = get(F, 2, 1)
    sigma = jax.nn.sigmoid(feats)
    turn = sigma * (1.0 + feats * (1.0 - sigma))
    put(og, 0, 0, get(C_, 0, 1) + conv_backward(G, V1) * turn)
    write_g = pltpu.make_async_copy(og, out_g, lsem.at[1])
    write_g.start()

    three_a = second_finish(0, two_a)
    three_b = second_finish(1, two_b)
    four_a = third_finish(0, three_a)
    four_b = third_finish(1, three_b)

    def give(g, copy, buffer, out):
        copy.wait_recv()
        for pair in range(14):
            values = D[g, pair // per_part, pair % per_part]
            if pair < 9:
                taps = (3 * pair, 3 * pair + 1)
            else:
                taps = (6 * (pair - 9) + 2, 6 * (pair - 9) + 5)
            for n, tap in enumerate(taps):
                if tap < 27:
                    buffer[tap] = values[n * oc : (n + 1) * oc]
        write = pltpu.make_async_copy(buffer, out, lsem.at[2 + g])
        write.start()
        return write

    write_1 = give(0, four_a, o1, out_1)
    write_2 = give(1, four_b, o2, out_2)
    for copy in sent:
        copy.wait_send()
    for write in (write_b, write_g, write_1, write_2):
        write.wait()


def build(geom, features, cotangent, first_kernel, second_kernel):
    nz, ny, nx, width, cells_all = geom
    FR, RT = features.shape[0], features.shape[1]
    ntm = nz * ny
    oc = C // ntm
    tall = 2 * oc
    cells = FR * RT * width
    pad = pltpu.VMEM((FR + 2, RT + 2, width, C), BF16)
    forward = pltpu.VMEM((3, 3, 4, C, 2 * C), BF16)
    backward = pltpu.VMEM((3, 3, 2 * C, 4 * C), BF16)
    nf, ns = ny, nz
    scratch = [
        pad, pad, pad, pad, pad,
        forward, backward, forward, backward,
        pltpu.VMEM((cells // 2, 2 * C), F32),
        pltpu.VMEM((3 * C, cells), BF16),
        pltpu.VMEM((2, 2, nf, ns, 7, tall, C), BF16),
        pltpu.VMEM((2, nf, ns, 7, tall, C), BF16),
        pltpu.VMEM((2, nf, ns, 7, tall, C), BF16),
        pltpu.VMEM((2, nf - 1, ns, 7, tall, C), BF16),
        pltpu.VMEM((2, ns, 7, tall, C), BF16),
        pltpu.VMEM((2, ns - 1, 7, tall, C), BF16),
        pltpu.VMEM((2, 7, tall, C), BF16),
        pltpu.VMEM((2, nx - 1, 7, tall, C), BF16),
        pltpu.VMEM((2, 2, 7, tall, C), F32),
        pltpu.VMEM((FR, RT, width, C), BF16),
        pltpu.VMEM((FR, RT, width, C), BF16),
        pltpu.VMEM((27, oc, C), F32),
        pltpu.VMEM((27, oc, C), F32),
        pltpu.SemaphoreType.DMA((50,)),
        pltpu.SemaphoreType.DMA((4,)),
        pltpu.SemaphoreType.DMA((4, 5)),
        pltpu.SemaphoreType.DMA((4, 5)),
        pltpu.SemaphoreType.DMA((2,)),
        pltpu.SemaphoreType.DMA((2,)),
        pltpu.SemaphoreType.DMA((2, nf - 1)),
        pltpu.SemaphoreType.DMA((2, nf - 1)),
        pltpu.SemaphoreType.DMA((2, ns - 1)),
        pltpu.SemaphoreType.DMA((2, ns - 1)),
        pltpu.SemaphoreType.DMA((2, nx - 1)),
        pltpu.SemaphoreType.DMA((2, nx - 1)),
        pltpu.SemaphoreType.DMA((2,)),
        pltpu.SemaphoreType.DMA((2,)),
    ]
    anywhere = pl.BlockSpec(memory_space=pl.ANY)
    field = jax.ShapeDtypeStruct(features.shape, BF16)
    grads = jax.ShapeDtypeStruct((27, oc, C), F32)
    block_out, grad_input, g1, g2 = pl.pallas_call(
        functools.partial(kernel, geom),
        out_shape=(field, field, grads, grads),
        in_specs=[anywhere] * 4,
        out_specs=(anywhere,) * 4,
        scratch_shapes=scratch,
        compiler_params=pltpu.CompilerParams(
            collective_id=0, has_side_effects=True, vmem_limit_bytes=48 * 1024 * 1024
        ),
    )(features, cotangent, first_kernel, second_kernel)

    def place(values):
        return jnp.transpose(values.reshape(3, 3, 3, oc, C), (0, 1, 2, 4, 3))

    return block_out, grad_input, place(g1), place(g2)


def solution(mesh, sides=(4, 4, 4)):
    nz, ny, nx = sides

    def on_device(features, cotangent, first_kernel, second_kernel):
        width = features.shape[2]
        cells_all = features.shape[0] * features.shape[1] * width * nz * ny * nx * 2
        geom = (nz, ny, nx, width, cells_all)
        return build(geom, features, cotangent, first_kernel, second_kernel)

    return jax.shard_map(
        on_device,
        mesh=mesh,
        in_specs=(P("tm", "rows", None, None), P("tm", "rows", None, None), P(), P()),
        out_specs=(
            P("tm", "rows", None, None),
            P("tm", "rows", None, None),
            P(None, None, None, None, "tm"),
            P(None, None, None, None, "tm"),
        ),
        check_vma=False,
    )
```

```python
import functools
import math

import jax
import jax.numpy as jnp
from jax import lax
from jax.experimental import pallas as pl
from jax.experimental.pallas import tpu as pltpu
from jax.sharding import PartitionSpec as P

C = 128
MESH = pl.DeviceIdType.MESH
F32 = jnp.float32
BF16 = jnp.bfloat16


def zero_shift(values, step, width):
    if step == 0:
        return values
    rows = values.shape[0]
    column = lax.broadcasted_iota(jnp.int32, values.shape, 0) % width
    rolled = pltpu.roll(values, (-step) % rows, 0)
    edge = width - 1 if step > 0 else 0
    return jnp.where(column == edge, 0.0, rolled)


def kernel(
    geom, feat, cot, k1, k2, out_b, out_g, out_1, out_2,
    F, X, C_, H, G, W1, V2, W2, V1, slope, LT, CT, CO, PP, R0, S1, R1, S2, R2, E, ob, og, o1, o2,
    wsem, lsem, hsend, hrecv, s0, r0, s1, r1, s2, r2, s3, r3,
):
    nz, ny, nx, width, cells_all = geom
    ntm, nrows = nz * ny, nx * 2
    oc = C // ntm
    FR, RT = feat.shape[0], feat.shape[1]
    pairs = RT // 2
    cells = FR * RT * width
    tm, rows = lax.axis_index("tm"), lax.axis_index("rows")
    z, y = tm // ny, tm % ny
    x, core = rows // 2, rows % 2
    nf, plane = nx, nz * ny
    first = (1 - core) * x + core * z
    beside = (1 - core) * z + core * x
    spot = beside * ny + y

    def first_peer(d):
        return ((1 - core) * tm + core * (((z + d) % nz) * ny + y), (1 - core) * (((x + d) % nx) * 2) + core * rows)

    def plane_spot(e):
        return ((beside + e // ny) % nz) * ny + (y + e % ny) % ny

    def plane_peer(e):
        to, at = (beside + e // ny) % nz, (y + e % ny) % ny
        return ((1 - core) * (to * ny + at) + core * (z * ny + at), (1 - core) * rows + core * (to * 2 + 1))

    up, down = (tm + 1) % ntm, (tm + ntm - 1) % ntm
    right, left = (rows + 1) % nrows, (rows + nrows - 1) % nrows
    partner = x * 2 + 1 - core

    loads = {}
    count = [0]

    def load(name, src, dst):
        copy = pltpu.make_async_copy(src, dst, wsem.at[count[0]])
        count[0] += 1
        copy.start()
        loads.setdefault(name, []).append(copy)

    def arrived(name):
        for copy in loads[name]:
            copy.wait()

    load("F", feat, F.at[2 : 2 + FR, 1 : 1 + RT])
    load("C", cot, C_.at[0:FR, 1 : 1 + RT])

    def load_forward(name, src, W):
        for k in range(3):
            for o in range(2):
                load(name, src.at[:, :, k], W.at[k, :, o : o + 3, :, o * C : (o + 1) * C])

    def load_backward(name, src, V):
        for k in range(3):
            for o in range(2):
                for j in range(3):
                    at = o + 2 - j
                    load(name, src.at[:, j, k], V.at[k, :, o * C : (o + 1) * C, at * C : (at + 1) * C])

    load_forward("W1", k1, W1)
    load_backward("V2", k2, V2)
    load_forward("W2", k2, W2)
    load_backward("V1", k1, V1)

    peers = [(up, rows), (up, right), (up, left), (down, rows), (down, right), (down, left)]
    peers += [(tm, (rows + o) % nrows) for o in range(1, nrows)]
    peers += [first_peer(d) for d in range(1, nf)]
    peers += [plane_peer(e) for e in range(1, plane)]
    barrier = pltpu.get_barrier_semaphore()
    for peer in peers:
        pl.semaphore_signal(barrier, inc=1, device_id=peer, device_id_type=MESH)
    pl.semaphore_wait(barrier, len(peers))

    def remote(src, dst, send, recv, peer):
        copy = pltpu.make_async_remote_copy(
            src_ref=src, dst_ref=dst, send_sem=send, recv_sem=recv, device_id=peer, device_id_type=MESH
        )
        copy.start()
        return copy

    sent = []

    def send_halo(which, src, at_f, at_r, dst, before):
        own = 2 if before else 0
        edge_src = slice(at_f + FR - 2, at_f + FR) if before else slice(at_f, at_f + 2)
        edge_dst = slice(0, 2) if before else slice(FR, FR + 2)
        ahead = up if before else down
        whole_src, whole_dst = slice(at_f, at_f + FR), slice(own, own + FR)
        last, start = slice(at_r + RT - 1, at_r + RT), slice(at_r, at_r + 1)
        low, high = slice(0, 1), slice(RT + 1, RT + 2)
        inner_src, inner_dst = slice(at_r, at_r + RT), slice(1, 1 + RT)
        plan = [
            (edge_src, inner_src, edge_dst, inner_dst, (ahead, rows)),
            (edge_src, last, edge_dst, low, (ahead, right)),
            (edge_src, start, edge_dst, high, (ahead, left)),
            (whole_src, last, whole_dst, low, (tm, right)),
            (whole_src, start, whole_dst, high, (tm, left)),
        ]
        copies = []
        for n, (sf, sr, df, dr, peer) in enumerate(plan):
            copies.append(remote(src.at[sf, sr], dst.at[df, dr], hsend.at[which, n], hrecv.at[which, n], peer))
        sent.extend(copies)
        return copies

    def receive_halo(copies, dst, before):
        for copy in copies:
            copy.wait_recv()

        @pl.when(tm == (0 if before else ntm - 1))
        def _():
            at = 0 if before else FR
            dst[at : at + 2] = jnp.zeros((2, RT + 2, width, C), BF16)

        @pl.when(rows == 0)
        def _():
            dst[:, 0] = jnp.zeros((FR + 2, width, C), BF16)

        @pl.when(rows == nrows - 1)
        def _():
            dst[:, RT + 1] = jnp.zeros((FR + 2, width, C), BF16)

    halo_f = send_halo(0, feat, 0, 0, F, True)
    halo_c = send_halo(1, cot, 0, 0, C_, False)

    for W in (W1, W2):
        W[:, :, 3, :, 0:C] = jnp.zeros((3, 3, C, C), BF16)
        W[:, :, 0, :, C : 2 * C] = jnp.zeros((3, 3, C, C), BF16)
    for V in (V1, V2):
        V[:, :, 0:C, 3 * C : 4 * C] = jnp.zeros((3, 3, C, C), BF16)
        V[:, :, C : 2 * C, 0:C] = jnp.zeros((3, 3, C, C), BF16)

    chunk = 8 // nx
    for g in range(2):
        PP[g, 0, nx - 1, :, chunk - 1] = jnp.zeros((plane, 2 * oc, C), BF16)
        PP[g, 1, :, (nx - 1) * ny :, chunk - 1] = jnp.zeros((nz, ny, 2 * oc, C), BF16)

    def sigmoid(values):
        return 0.5 * jnp.tanh(0.5 * values) + 0.5

    def silu_into(f, r):
        feats = F[f, r].astype(F32)
        X[f, r] = (feats * sigmoid(feats)).astype(BF16)

    arrived("F")
    for f in range(2, 2 + FR):
        silu_into(f, slice(1, 1 + RT))

    def window(field, lead):
        parts = []
        for pair in range(pairs):
            blocks = []
            for i in lead:
                for r in range(4):
                    blocks.append(field[i : i + FR, 2 * pair + r].reshape(FR * width, C))
            parts.append(jnp.concatenate(blocks, axis=1))
        return jnp.concatenate(parts, axis=0)

    def conv_forward(field, W):
        lhs = window(field, (0, 1, 2))
        total = None
        for k in (1, 0, 2):
            got = jnp.dot(lhs, W[k].reshape(12 * C, 2 * C), preferred_element_type=F32)
            got = zero_shift(got, k - 1, width)
            total = got if total is None else total + got
        return total

    def conv_backward(field, V):
        lhs = window(field, (2, 1, 0))
        total = None
        for k in (1, 0, 2):
            rhs = jnp.concatenate([V[k, i] for i in range(3)], axis=1)
            got = lax.dot_general(lhs, rhs, (((1,), (1,)), ((), ())), preferred_element_type=F32)
            got = zero_shift(got, 1 - k, width)
            total = got if total is None else total + got
        return total

    def put(dst, at_f, at_r, values):
        for pair in range(pairs):
            for o in range(2):
                part = values[pair * FR * width : (pair + 1) * FR * width, o * C : (o + 1) * C]
                dst[at_f : at_f + FR, at_r + 2 * pair + o] = part.reshape(FR, width, C).astype(dst.dtype)

    def get(src, at_f, at_r):
        parts = []
        for pair in range(pairs):
            blocks = [src[at_f : at_f + FR, at_r + 2 * pair + o].reshape(FR * width, C) for o in range(2)]
            parts.append(jnp.concatenate(blocks, axis=1))
        return jnp.concatenate(parts, axis=0).astype(F32)

    receive_halo(halo_f, F, True)
    for f in range(2):
        silu_into(f, slice(0, RT + 2))
    for f in range(2, 2 + FR):
        silu_into(f, slice(0, 1))
        silu_into(f, slice(RT + 1, RT + 2))
    arrived("W1")
    first_out = conv_forward(X, W1)
    sigma = sigmoid(first_out)
    put(H, 2, 1, first_out * sigma)
    slope[...] = sigma * (1.0 + first_out * (1.0 - sigma))
    halo_h = send_halo(2, H, 2, 1, H, True)

    eye = (
        lax.broadcasted_iota(jnp.int32, (C, C), 0) == lax.broadcasted_iota(jnp.int32, (C, C), 1)
    ).astype(BF16)
    per_part = 7
    spots = [(i, j) for i in range(3) for j in range(3)]

    def turned(values):
        return lax.dot_general(eye, values, (((1,), (1,)), ((), ())), preferred_element_type=F32).astype(BF16)

    def store(g, pair, a, b):
        part, slot = pair // per_part, pair % per_part
        xs, at = slot // chunk, slot % chunk
        both = jnp.concatenate([a.reshape(ntm, oc, C), b.reshape(ntm, oc, C)], axis=1).astype(BF16)
        if part == 0:
            PP[g, 0, xs, :, at] = both
        else:
            for zz in range(nz):
                PP[g, 1, zz, xs * ny : (xs + 1) * ny, at] = both[zz * ny : (zz + 1) * ny]

    def store_third(g, thirds):
        thirds = thirds + [jnp.zeros((C, C), F32)]
        for m in range(5):
            store(g, 9 + m, thirds[2 * m], thirds[2 * m + 1])

    def first_kernel_gradient():
        grads = G[0:FR, 1 : 1 + RT].reshape(cells, C).astype(F32)
        for k in range(3):
            LT[k * C : (k + 1) * C] = turned(zero_shift(grads, 1 - k, width).astype(BF16))
        thirds = []
        for m in range(5):
            group = spots[2 * m : 2 * m + 2]
            rhs = jnp.concatenate([X[i : i + FR, j : j + RT].reshape(cells, C) for i, j in group], axis=1)
            got = jnp.dot(LT[...], rhs, preferred_element_type=F32)
            for n in range(len(group)):
                side = got[:, n * C : (n + 1) * C]
                store(0, 2 * m + n, side[0:C], side[C : 2 * C])
                thirds.append(side[2 * C : 3 * C])
        store_third(0, thirds)

    def second_kernel_gradient():
        tall = (RT + 2) * width
        for f in range(FR + 2):
            CT[:, f * tall : (f + 1) * tall] = turned(C_[f].reshape(tall, C))
            CO[:, f * RT * width : (f + 1) * RT * width] = turned(C_[f, 1 : 1 + RT].reshape(RT * width, C))
        hidden = H[2 : 2 + FR, 1 : 1 + RT].reshape(cells, C).astype(F32)
        rhs = jnp.concatenate([zero_shift(hidden, k - 1, width).astype(BF16) for k in range(3)], axis=1)

        def turned_window(a, b):
            if b == 1:
                return CO[:, a * RT * width : (a + FR) * RT * width]
            return jnp.concatenate(
                [CT[:, f * tall + b * width : f * tall + (b + RT) * width] for f in range(a, a + FR)], axis=1
            )

        thirds = []
        for i in range(3):
            lhs = jnp.concatenate([turned_window(2 - i, 2 - j) for j in range(3)], axis=0)
            got = jnp.dot(lhs, rhs, preferred_element_type=F32)
            for j in range(3):
                side = got[j * C : (j + 1) * C]
                store(1, 3 * i + j, side[:, 0:C], side[:, C : 2 * C])
                thirds.append(side[:, 2 * C : 3 * C])
        store_third(1, thirds)

    order = list(range(1, nf)) + [0]
    other_first = (1 - core) * z + core * x

    def pair_start(g):
        copies = []
        for d in order:
            at = (other_first + d) % nf
            copies.append(remote(PP.at[g, 1 - core, at], R0.at[g, at], s0.at[g, d], r0.at[g, d], (tm, partner)))
        sent.extend(copies)
        return copies

    def pair_finish(g, copies):
        more = []
        for d, copy in zip(order, copies):
            at = (first + d) % nf
            pltpu.make_async_remote_copy(
                src_ref=PP.at[g, core, at], dst_ref=R0.at[g, at], send_sem=s0.at[g, d], recv_sem=r0.at[g, d],
                device_id=(tm, partner), device_id_type=MESH,
            ).wait_recv()
            S1[g, at] = (PP[g, core, at].astype(F32) + R0[g, at].astype(F32)).astype(BF16)
            if d:
                more.append(remote(S1.at[g, at], R1.at[g, d - 1], s1.at[g, d - 1], r1.at[g, d - 1], first_peer(d)))
        sent.extend(more)
        return more

    def first_finish(g, copies):
        for copy in copies:
            copy.wait_recv()
        total = S1[g, first].astype(F32)
        for d in range(1, nf):
            total = total + R1[g, d - 1].astype(F32)
        S2[g] = total.astype(BF16)
        more = [
            remote(S2.at[g, plane_spot(e)], R2.at[g, e - 1], s2.at[g, e - 1], r2.at[g, e - 1], plane_peer(e))
            for e in range(1, plane)
        ]
        sent.extend(more)
        return more

    scale = 1.0 / math.sqrt(cells_all)

    def plane_finish(g, copies):
        for copy in copies:
            copy.wait_recv()
        total = S2[g, spot].astype(F32)
        for e in range(1, plane):
            total = total + R2[g, e - 1].astype(F32)
        E[g, core, x] = (total * scale).astype(BF16)
        more = [
            remote(
                E.at[g, core, x], E.at[g, core, x], s3.at[g, o - 1], r3.at[g, o - 1], (tm, (rows + o) % nrows)
            )
            for o in range(1, nrows)
        ]
        sent.extend(more)
        return more

    def give(g, copies, buffer, out):
        for o in range(1, nrows):
            giver = (rows + nrows - o) % nrows
            block = E.at[g, giver % 2, giver // 2]
            pltpu.make_async_remote_copy(
                src_ref=block, dst_ref=block, send_sem=s3.at[g, o - 1], recv_sem=r3.at[g, o - 1],
                device_id=(tm, (rows + o) % nrows), device_id_type=MESH,
            ).wait_recv()
        for pair in range(14):
            slot = pair % per_part
            values = E[g, pair // per_part, slot // chunk, slot % chunk].astype(F32)
            if pair < 9:
                taps = (3 * pair, 3 * pair + 1)
            else:
                taps = (6 * (pair - 9) + 2, 6 * (pair - 9) + 5)
            for n, tap in enumerate(taps):
                if tap < 27:
                    buffer[tap] = values[n * oc : (n + 1) * oc]
        write = pltpu.make_async_copy(buffer, out, lsem.at[2 + g])
        write.start()
        return write

    arrived("C")
    receive_halo(halo_c, C_, False)
    second_kernel_gradient()
    pair_b = pair_start(1)

    arrived("V2")
    put(G, 0, 1, conv_backward(C_, V2) * slope[...])
    halo_g = send_halo(3, G, 0, 1, G, False)
    one_b = pair_finish(1, pair_b)
    first_kernel_gradient()
    pair_a = pair_start(0)
    two_b = first_finish(1, one_b)
    one_a = pair_finish(0, pair_a)

    receive_halo(halo_h, H, True)
    arrived("W2")
    put(ob, 0, 0, get(F, 2, 1) + conv_forward(H, W2))
    write_b = pltpu.make_async_copy(ob, out_b, lsem.at[0])
    write_b.start()

    three_b = plane_finish(1, two_b)
    two_a = first_finish(0, one_a)

    receive_halo(halo_g, G, False)
    arrived("V1")
    feats = get(F, 2, 1)
    sigma = sigmoid(feats)
    turn = sigma * (1.0 + feats * (1.0 - sigma))
    put(og, 0, 0, get(C_, 0, 1) + conv_backward(G, V1) * turn)
    write_g = pltpu.make_async_copy(og, out_g, lsem.at[1])
    write_g.start()

    three_a = plane_finish(0, two_a)
    write_2 = give(1, three_b, o2, out_2)
    write_1 = give(0, three_a, o1, out_1)
    for copy in sent:
        copy.wait_send()
    for write in (write_b, write_g, write_1, write_2):
        write.wait()


def hand_out(a, b, c, d, out_a, out_b, out_c, out_d, sems):
    pairs = ((a, out_a), (b, out_b), (c, out_c), (d, out_d))
    copies = [pltpu.make_async_copy(src, dst, sems.at[n]) for n, (src, dst) in enumerate(pairs)]
    for copy in copies:
        copy.start()
    for copy in copies:
        copy.wait()


def build(geom, features, cotangent, first_kernel, second_kernel):
    nz, ny, nx, width, cells_all = geom
    FR, RT = features.shape[0], features.shape[1]
    ntm = nz * ny
    oc = C // ntm
    tall = 2 * oc
    cells = FR * RT * width
    pad = pltpu.VMEM((FR + 2, RT + 2, width, C), BF16)
    forward = pltpu.VMEM((3, 3, 4, C, 2 * C), BF16)
    backward = pltpu.VMEM((3, 3, 2 * C, 4 * C), BF16)
    nf, plane, chunk = nx, nz * ny, 8 // nx
    scratch = [
        pad, pad, pad, pad, pad,
        forward, backward, forward, backward,
        pltpu.VMEM((cells // 2, 2 * C), F32),
        pltpu.VMEM((3 * C, cells), BF16),
        pltpu.VMEM((C, (FR + 2) * (RT + 2) * width), BF16),
        pltpu.VMEM((C, (FR + 2) * RT * width), BF16),
        pltpu.VMEM((2, 2, nf, plane, chunk, tall, C), BF16),
        pltpu.VMEM((2, nf, plane, chunk, tall, C), BF16),
        pltpu.VMEM((2, nf, plane, chunk, tall, C), BF16),
        pltpu.VMEM((2, nf - 1, plane, chunk, tall, C), BF16),
        pltpu.VMEM((2, plane, chunk, tall, C), BF16),
        pltpu.VMEM((2, plane - 1, chunk, tall, C), BF16),
        pltpu.VMEM((2, 2, nx, chunk, tall, C), BF16),
        pltpu.VMEM((FR, RT, width, C), BF16),
        pltpu.VMEM((FR, RT, width, C), BF16),
        pltpu.VMEM((27, oc, C), F32),
        pltpu.VMEM((27, oc, C), F32),
        pltpu.SemaphoreType.DMA((50,)),
        pltpu.SemaphoreType.DMA((4,)),
        pltpu.SemaphoreType.DMA((4, 5)),
        pltpu.SemaphoreType.DMA((4, 5)),
        pltpu.SemaphoreType.DMA((2, nf)),
        pltpu.SemaphoreType.DMA((2, nf)),
        pltpu.SemaphoreType.DMA((2, nf - 1)),
        pltpu.SemaphoreType.DMA((2, nf - 1)),
        pltpu.SemaphoreType.DMA((2, plane - 1)),
        pltpu.SemaphoreType.DMA((2, plane - 1)),
        pltpu.SemaphoreType.DMA((2, 2 * nx - 1)),
        pltpu.SemaphoreType.DMA((2, 2 * nx - 1)),
    ]
    anywhere = pl.BlockSpec(memory_space=pl.ANY)
    features, cotangent, first_kernel, second_kernel = [
        pltpu.with_memory_space_constraint(value, pltpu.HBM)
        for value in (features, cotangent, first_kernel, second_kernel)
    ]
    field = jax.ShapeDtypeStruct(features.shape, BF16)
    grads = jax.ShapeDtypeStruct((27, oc, C), F32)
    block_out, grad_input, g1, g2 = pl.pallas_call(
        functools.partial(kernel, geom),
        out_shape=(field, field, grads, grads),
        in_specs=[anywhere] * 4,
        out_specs=(anywhere,) * 4,
        scratch_shapes=scratch,
        compiler_params=pltpu.CompilerParams(
            collective_id=0, has_side_effects=True, vmem_limit_bytes=48 * 1024 * 1024
        ),
    )(features, cotangent, first_kernel, second_kernel)

    block_out, grad_input, g1, g2 = pl.pallas_call(
        hand_out,
        out_shape=(field, field, grads, grads),
        in_specs=[anywhere] * 4,
        out_specs=(anywhere,) * 4,
        scratch_shapes=[pltpu.SemaphoreType.DMA((4,))],
        compiler_params=pltpu.CompilerParams(vmem_limit_bytes=8 * 1024 * 1024),
    )(block_out, grad_input, g1, g2)

    def place(values):
        return jnp.transpose(values.reshape(3, 3, 3, oc, C), (0, 1, 2, 4, 3))

    return block_out, grad_input, place(g1), place(g2)


def solution(mesh, sides=(4, 4, 4)):
    nz, ny, nx = sides

    def on_device(features, cotangent, first_kernel, second_kernel):
        width = features.shape[2]
        cells_all = features.shape[0] * features.shape[1] * width * nz * ny * nx * 2
        geom = (nz, ny, nx, width, cells_all)
        return build(geom, features, cotangent, first_kernel, second_kernel)

    return jax.shard_map(
        on_device,
        mesh=mesh,
        in_specs=(P("tm", "rows", None, None), P("tm", "rows", None, None), P(), P()),
        out_specs=(
            P("tm", "rows", None, None),
            P("tm", "rows", None, None),
            P(None, None, None, None, "tm"),
            P(None, None, None, None, "tm"),
        ),
        check_vma=False,
    )
```

```python
import functools
import math

import jax
import jax.numpy as jnp
from jax import lax
from jax.experimental import pallas as pl
from jax.experimental.pallas import tpu as pltpu
from jax.sharding import PartitionSpec as P

C = 128
MESH = pl.DeviceIdType.MESH
F32 = jnp.float32
BF16 = jnp.bfloat16


def zero_shift(values, step, width):
    if step == 0:
        return values
    rows = values.shape[0]
    column = lax.broadcasted_iota(jnp.int32, values.shape, 0) % width
    rolled = pltpu.roll(values, (-step) % rows, 0)
    edge = width - 1 if step > 0 else 0
    return jnp.where(column == edge, 0.0, rolled)


def kernel(
    geom, feat, cot, k1, k2, out_b, out_g, out_1, out_2,
    F, X, C_, H, G, W1, V2, W2, V1, slope, early, LT, CT, CO, PP, R0, S1, R1, E,
    wsem, hsend, hrecv, s0, r0, s1, r1, s2, r2,
):
    nz, ny, nx, width, cells_all = geom
    ntm, nrows = nz * ny, nx * 2
    oc = C // ntm
    FR, RT = feat.shape[0], feat.shape[1]
    pairs = RT // 2
    cells = FR * RT * width
    tm, rows = lax.axis_index("tm"), lax.axis_index("rows")
    z, y = tm // ny, tm % ny
    x, core = rows // 2, rows % 2
    up, down = (tm + 1) % ntm, (tm + ntm - 1) % ntm
    right, left = (rows + 1) % nrows, (rows + nrows - 1) % nrows
    partner = x * 2 + 1 - core

    loads = {}
    count = [0]

    def load(name, src, dst):
        copy = pltpu.make_async_copy(src, dst, wsem.at[count[0]])
        count[0] += 1
        copy.start()
        loads.setdefault(name, []).append(copy)

    def arrived(name):
        for copy in loads[name]:
            copy.wait()

    load("F", feat, F.at[2 : 2 + FR, 1 : 1 + RT])
    load("C", cot, C_.at[0:FR, 1 : 1 + RT])

    def load_forward(name, src, W):
        for k in range(3):
            for o in range(2):
                load(name, src.at[:, :, k], W.at[k, :, o : o + 3, :, o * C : (o + 1) * C])

    def load_backward(name, src, V):
        for k in range(3):
            for o in range(2):
                for j in range(3):
                    at = o + 2 - j
                    load(name, src.at[:, j, k], V.at[k, :, o * C : (o + 1) * C, at * C : (at + 1) * C])

    load_forward("W1", k1, W1)
    load_backward("V2", k2, V2)
    load_forward("W2", k2, W2)
    load_backward("V1", k1, V1)

    peers = [(up, right), (up, left), (down, right), (down, left)]
    peers += [(tm, (rows + o) % nrows) for o in range(1, nrows)]

    def plane_peer(dz, dy):
        return (((z + dz) % nz) * ny + (y + dy) % ny, rows)

    offsets = [(dz, dy) for dz in list(range(1, nz)) + [0] for dy in range(ny) if (dz, dy) != (0, 0)]
    peers += [plane_peer(dz, dy) for dz, dy in offsets]
    barrier = pltpu.get_barrier_semaphore()
    for peer in peers:
        pl.semaphore_signal(barrier, inc=1, device_id=peer, device_id_type=MESH)
    pl.semaphore_wait(barrier, len(peers))

    def remote(src, dst, send, recv, peer):
        copy = pltpu.make_async_remote_copy(
            src_ref=src, dst_ref=dst, send_sem=send, recv_sem=recv, device_id=peer, device_id_type=MESH
        )
        copy.start()
        return copy

    sent = []

    def send_rows(which, src, at_f, at_r, dst, before):
        own = 2 if before else 0
        frames_src, frames_dst = slice(at_f, at_f + FR), slice(own, own + FR)
        plan = [
            (slice(at_r + RT - 1, at_r + RT), slice(0, 1), (tm, right)),
            (slice(at_r, at_r + 1), slice(RT + 1, RT + 2), (tm, left)),
        ]
        copies = []
        for n, (sr, dr, peer) in enumerate(plan):
            copies.append(
                remote(src.at[frames_src, sr], dst.at[frames_dst, dr], hsend.at[which, n], hrecv.at[which, n], peer)
            )
        sent.extend(copies)
        return copies

    def send_time(which, src, at_f, at_r, dst, before):
        frames_src = slice(at_f + FR - 2, at_f + FR) if before else slice(at_f, at_f + 2)
        frames_dst = slice(0, 2) if before else slice(FR, FR + 2)
        ahead = up if before else down
        plan = [
            (slice(at_r, at_r + RT), slice(1, 1 + RT), (ahead, rows)),
            (slice(at_r + RT - 1, at_r + RT), slice(0, 1), (ahead, right)),
            (slice(at_r, at_r + 1), slice(RT + 1, RT + 2), (ahead, left)),
        ]
        copies = []
        for n, (sr, dr, peer) in enumerate(plan):
            copies.append(
                remote(
                    src.at[frames_src, sr], dst.at[frames_dst, dr], hsend.at[which, 2 + n], hrecv.at[which, 2 + n], peer
                )
            )
        sent.extend(copies)
        return copies

    def clear_rims(dst, frames, count):
        @pl.when(rows == 0)
        def _():
            dst[frames, 0] = jnp.zeros((count, width, C), BF16)

        @pl.when(rows == nrows - 1)
        def _():
            dst[frames, RT + 1] = jnp.zeros((count, width, C), BF16)

    def receive_rows(copies, dst, before):
        for copy in copies:
            copy.wait_recv()
        own = 2 if before else 0
        clear_rims(dst, slice(own, own + FR), FR)

    def receive_time(copies, dst, before):
        for copy in copies:
            copy.wait_recv()
        at = 0 if before else FR

        @pl.when(tm == (0 if before else ntm - 1))
        def _():
            dst[at : at + 2] = jnp.zeros((2, RT + 2, width, C), BF16)

        clear_rims(dst, slice(at, at + 2), 2)

    rows_f = send_rows(0, feat, 0, 0, F, True)
    rows_c = send_rows(1, cot, 0, 0, C_, False)
    time_f = send_time(0, feat, 0, 0, F, True)
    time_c = send_time(1, cot, 0, 0, C_, False)

    for W in (W1, W2):
        W[:, :, 3, :, 0:C] = jnp.zeros((3, 3, C, C), BF16)
        W[:, :, 0, :, C : 2 * C] = jnp.zeros((3, 3, C, C), BF16)
    for V in (V1, V2):
        V[:, :, 0:C, 3 * C : 4 * C] = jnp.zeros((3, 3, C, C), BF16)
        V[:, :, C : 2 * C, 0:C] = jnp.zeros((3, 3, C, C), BF16)

    def sigmoid(values):
        return 0.5 * jnp.tanh(0.5 * values) + 0.5

    def silu_into(f, r):
        feats = F[f, r].astype(F32)
        X[f, r] = (feats * sigmoid(feats)).astype(BF16)

    arrived("F")
    for f in range(2, 2 + FR):
        silu_into(f, slice(1, 1 + RT))

    half = FR // 2

    def window(field, lead, lo, count):
        parts = []
        for pair in range(pairs):
            blocks = []
            for i in lead:
                for r in range(4):
                    blocks.append(field[lo + i : lo + i + count, 2 * pair + r].reshape(count * width, C))
            parts.append(jnp.concatenate(blocks, axis=1))
        return jnp.concatenate(parts, axis=0)

    def conv_forward(field, W, lo, count):
        lhs = window(field, (0, 1, 2), lo, count)
        total = None
        for k in (1, 0, 2):
            got = jnp.dot(lhs, W[k].reshape(12 * C, 2 * C), preferred_element_type=F32)
            got = zero_shift(got, k - 1, width)
            total = got if total is None else total + got
        return total

    def conv_backward(field, V, lo, count):
        lhs = window(field, (2, 1, 0), lo, count)
        total = None
        for k in (1, 0, 2):
            rhs = jnp.concatenate([V[k, i] for i in range(3)], axis=1)
            got = lax.dot_general(lhs, rhs, (((1,), (1,)), ((), ())), preferred_element_type=F32)
            got = zero_shift(got, 1 - k, width)
            total = got if total is None else total + got
        return total

    def put(dst, at_f, at_r, values):
        deep = values.shape[0] // pairs
        count = deep // width
        for pair in range(pairs):
            for o in range(2):
                part = values[pair * deep : (pair + 1) * deep, o * C : (o + 1) * C]
                dst[at_f : at_f + count, at_r + 2 * pair + o] = part.reshape(count, width, C).astype(dst.dtype)

    def get(src, at_f, at_r, count):
        parts = []
        for pair in range(pairs):
            blocks = [src[at_f : at_f + count, at_r + 2 * pair + o].reshape(count * width, C) for o in range(2)]
            parts.append(jnp.concatenate(blocks, axis=1))
        return jnp.concatenate(parts, axis=0).astype(F32)

    def first_conv(part):
        first_out = conv_forward(X, W1, part * half, half)
        sigma = sigmoid(first_out)
        put(H, 2 + part * half, 1, first_out * sigma)
        slope[part] = sigma * (1.0 + first_out * (1.0 - sigma))

    eye = (
        lax.broadcasted_iota(jnp.int32, (C, C), 0) == lax.broadcasted_iota(jnp.int32, (C, C), 1)
    ).astype(BF16)
    per_part = 7
    spots = [(i, j) for i in range(3) for j in range(3)]

    def turned(values):
        return lax.dot_general(eye, values, (((1,), (1,)), ((), ())), preferred_element_type=F32).astype(BF16)

    def store(g, pair, a, b):
        part, slot = pair // per_part, pair % per_part
        both = jnp.concatenate([a.reshape(nz, ny, oc, C), b.reshape(nz, ny, oc, C)], axis=2).astype(BF16)
        PP[g, part, :, :, slot] = both

    def store_third(g, thirds):
        thirds = thirds + [jnp.zeros((C, C), F32)]
        for m in range(5):
            store(g, 9 + m, thirds[2 * m], thirds[2 * m + 1])

    def first_kernel_gradient():
        grads = G[0:FR, 1 : 1 + RT].reshape(cells, C).astype(F32)
        for k in range(3):
            LT[k * C : (k + 1) * C] = turned(zero_shift(grads, 1 - k, width).astype(BF16))
        thirds = []
        for m in range(5):
            group = spots[2 * m : 2 * m + 2]
            rhs = jnp.concatenate([X[i : i + FR, j : j + RT].reshape(cells, C) for i, j in group], axis=1)
            got = jnp.dot(LT[...], rhs, preferred_element_type=F32)
            for n in range(len(group)):
                side = got[:, n * C : (n + 1) * C]
                store(0, 2 * m + n, side[0:C], side[C : 2 * C])
                thirds.append(side[2 * C : 3 * C])
        store_third(0, thirds)

    def second_kernel_gradient():
        tall = (RT + 2) * width
        for f in range(FR + 2):
            CT[:, f * tall : (f + 1) * tall] = turned(C_[f].reshape(tall, C))
            CO[:, f * RT * width : (f + 1) * RT * width] = turned(C_[f, 1 : 1 + RT].reshape(RT * width, C))
        hidden = H[2 : 2 + FR, 1 : 1 + RT].reshape(cells, C).astype(F32)
        rhs = jnp.concatenate([zero_shift(hidden, k - 1, width).astype(BF16) for k in range(3)], axis=1)

        def turned_window(a, b):
            if b == 1:
                return CO[:, a * RT * width : (a + FR) * RT * width]
            return jnp.concatenate(
                [CT[:, f * tall + b * width : f * tall + (b + RT) * width] for f in range(a, a + FR)], axis=1
            )

        thirds = []
        for i in range(3):
            lhs = jnp.concatenate([turned_window(2 - i, 2 - j) for j in range(3)], axis=0)
            got = jnp.dot(lhs, rhs, preferred_element_type=F32)
            for j in range(3):
                side = got[j * C : (j + 1) * C]
                store(1, 3 * i + j, side[:, 0:C], side[:, C : 2 * C])
                thirds.append(side[:, 2 * C : 3 * C])
        store_third(1, thirds)

    order = list(range(1, nz)) + [0]

    def pair_start(g):
        copies = []
        for dz in order:
            at = (z + dz) % nz
            copies.append(remote(PP.at[g, 1 - core, at], R0.at[g, at], s0.at[g, dz], r0.at[g, dz], (tm, partner)))
        sent.extend(copies)
        return copies

    def pair_finish(g, copies):
        more = []
        for dz, copy in zip(order, copies):
            copy.wait_recv()
            at = (z + dz) % nz
            S1[g, at] = (PP[g, core, at].astype(F32) + R0[g, at].astype(F32)).astype(BF16)
            for dy in range(ny):
                if (dz, dy) == (0, 0):
                    continue
                e = dz * ny + dy - 1
                more.append(
                    remote(S1.at[g, at, (y + dy) % ny], R1.at[g, e], s1.at[g, e], r1.at[g, e], plane_peer(dz, dy))
                )
        sent.extend(more)
        return more

    scale = 1.0 / math.sqrt(cells_all)

    def plane_finish(g, copies):
        for copy in copies:
            copy.wait_recv()
        total = S1[g, z, y].astype(F32)
        for e in range(ntm - 1):
            total = total + R1[g, e].astype(F32)
        E[g, core, x] = total.astype(BF16)
        more = [
            remote(
                E.at[g, core, x], E.at[g, core, x], s2.at[g, o - 1], r2.at[g, o - 1], (tm, (rows + o) % nrows)
            )
            for o in range(1, nrows)
        ]
        sent.extend(more)
        return more

    def give(g, out):
        for o in range(1, nrows):
            giver = (rows + nrows - o) % nrows
            block = E.at[g, giver % 2, giver // 2]
            pltpu.make_async_remote_copy(
                src_ref=block, dst_ref=block, send_sem=s2.at[g, o - 1], recv_sem=r2.at[g, o - 1],
                device_id=(tm, (rows + o) % nrows), device_id_type=MESH,
            ).wait_recv()
        for pair in range(14):
            part, slot = pair // per_part, pair % per_part
            values = E[g, part, 0, slot].astype(F32)
            for at in range(1, nx):
                values = values + E[g, part, at, slot].astype(F32)
            values = values * scale
            if pair < 9:
                taps = (3 * pair, 3 * pair + 1)
            else:
                taps = (6 * (pair - 9) + 2, 6 * (pair - 9) + 5)
            for n, tap in enumerate(taps):
                if tap < 27:
                    out[tap] = values[n * oc : (n + 1) * oc]

    receive_rows(rows_f, F, True)
    for f in range(2, 2 + FR):
        silu_into(f, slice(0, 1))
        silu_into(f, slice(RT + 1, RT + 2))
    arrived("W1")
    first_conv(1)
    time_h = send_time(2, H, 2, 1, H, True)
    arrived("C")
    receive_rows(rows_c, C_, False)
    arrived("V2")
    early[...] = conv_backward(C_, V2, 0, half)

    receive_time(time_f, F, True)
    for f in range(2):
        silu_into(f, slice(0, RT + 2))
    first_conv(0)
    rows_h = send_rows(2, H, 2, 1, H, True)
    put(G, 0, 1, early[...] * slope[0])
    time_g = send_time(3, G, 0, 1, G, False)

    receive_time(time_c, C_, False)
    second_kernel_gradient()
    pair_b = pair_start(1)
    put(G, half, 1, conv_backward(C_, V2, half, half) * slope[1])
    rows_g = send_rows(3, G, 0, 1, G, False)
    plane_b = pair_finish(1, pair_b)
    first_kernel_gradient()
    pair_a = pair_start(0)
    plane_a = pair_finish(0, pair_a)

    receive_rows(rows_h, H, True)
    receive_time(time_h, H, True)
    arrived("W2")
    put(out_b, 0, 0, get(F, 2, 1, FR) + conv_forward(H, W2, 0, FR))

    rows_b = plane_finish(1, plane_b)

    receive_rows(rows_g, G, False)
    receive_time(time_g, G, False)
    arrived("V1")
    feats = get(F, 2, 1, FR)
    sigma = sigmoid(feats)
    turn = sigma * (1.0 + feats * (1.0 - sigma))
    put(out_g, 0, 0, get(C_, 0, 1, FR) + conv_backward(G, V1, 0, FR) * turn)

    rows_a = plane_finish(0, plane_a)
    give(1, out_2)
    give(0, out_1)
    for copy in sent:
        copy.wait_send()


def hand_out(a, b, c, d, out_a, out_b, out_c, out_d, sems):
    pairs = ((a, out_a), (b, out_b), (c, out_c), (d, out_d))
    copies = [pltpu.make_async_copy(src, dst, sems.at[n]) for n, (src, dst) in enumerate(pairs)]
    for copy in copies:
        copy.start()
    for copy in copies:
        copy.wait()


def build(geom, features, cotangent, first_kernel, second_kernel):
    nz, ny, nx, width, cells_all = geom
    FR, RT = features.shape[0], features.shape[1]
    ntm = nz * ny
    oc = C // ntm
    tall = 2 * oc
    cells = FR * RT * width
    pad = pltpu.VMEM((FR + 2, RT + 2, width, C), BF16)
    forward = pltpu.VMEM((3, 3, 4, C, 2 * C), BF16)
    backward = pltpu.VMEM((3, 3, 2 * C, 4 * C), BF16)
    block = (7, tall, C)
    scratch = [
        pad, pad, pad, pad, pad,
        forward, backward, forward, backward,
        pltpu.VMEM((2, cells // 4, 2 * C), F32),
        pltpu.VMEM((cells // 4, 2 * C), F32),
        pltpu.VMEM((3 * C, cells), BF16),
        pltpu.VMEM((C, (FR + 2) * (RT + 2) * width), BF16),
        pltpu.VMEM((C, (FR + 2) * RT * width), BF16),
        pltpu.VMEM((2, 2, nz, ny) + block, BF16),
        pltpu.VMEM((2, nz, ny) + block, BF16),
        pltpu.VMEM((2, nz, ny) + block, BF16),
        pltpu.VMEM((2, ntm - 1) + block, BF16),
        pltpu.VMEM((2, 2, nx) + block, BF16),
        pltpu.SemaphoreType.DMA((50,)),
        pltpu.SemaphoreType.DMA((4, 5)),
        pltpu.SemaphoreType.DMA((4, 5)),
        pltpu.SemaphoreType.DMA((2, nz)),
        pltpu.SemaphoreType.DMA((2, nz)),
        pltpu.SemaphoreType.DMA((2, ntm - 1)),
        pltpu.SemaphoreType.DMA((2, ntm - 1)),
        pltpu.SemaphoreType.DMA((2, 2 * nx - 1)),
        pltpu.SemaphoreType.DMA((2, 2 * nx - 1)),
    ]
    anywhere = pl.BlockSpec(memory_space=pl.ANY)
    features, cotangent, first_kernel, second_kernel = [
        pltpu.with_memory_space_constraint(value, pltpu.HBM)
        for value in (features, cotangent, first_kernel, second_kernel)
    ]
    field = jax.ShapeDtypeStruct(features.shape, BF16)
    grads = jax.ShapeDtypeStruct((27, oc, C), F32)
    block_out, grad_input, g1, g2 = pl.pallas_call(
        functools.partial(kernel, geom),
        out_shape=(field, field, grads, grads),
        in_specs=[anywhere] * 4,
        out_specs=(pl.BlockSpec(memory_space=pltpu.VMEM),) * 4,
        scratch_shapes=scratch,
        compiler_params=pltpu.CompilerParams(
            collective_id=0, has_side_effects=True, vmem_limit_bytes=48 * 1024 * 1024
        ),
    )(features, cotangent, first_kernel, second_kernel)

    block_out, grad_input, g1, g2 = pl.pallas_call(
        hand_out,
        out_shape=(field, field, grads, grads),
        in_specs=[anywhere] * 4,
        out_specs=(anywhere,) * 4,
        scratch_shapes=[pltpu.SemaphoreType.DMA((4,))],
        compiler_params=pltpu.CompilerParams(vmem_limit_bytes=8 * 1024 * 1024),
    )(block_out, grad_input, g1, g2)

    def place(values):
        return jnp.transpose(values.reshape(3, 3, 3, oc, C), (0, 1, 2, 4, 3))

    return block_out, grad_input, place(g1), place(g2)


def solution(mesh, sides=(4, 4, 4)):
    nz, ny, nx = sides

    def on_device(features, cotangent, first_kernel, second_kernel):
        width = features.shape[2]
        cells_all = features.shape[0] * features.shape[1] * width * nz * ny * nx * 2
        geom = (nz, ny, nx, width, cells_all)
        return build(geom, features, cotangent, first_kernel, second_kernel)

    return jax.shard_map(
        on_device,
        mesh=mesh,
        in_specs=(P("tm", "rows", None, None), P("tm", "rows", None, None), P(), P()),
        out_specs=(
            P("tm", "rows", None, None),
            P("tm", "rows", None, None),
            P(None, None, None, None, "tm"),
            P(None, None, None, None, "tm"),
        ),
        check_vma=False,
    )
```

```python
import functools
import math

import jax
import jax.numpy as jnp
from jax import lax
from jax.experimental import pallas as pl
from jax.experimental.pallas import tpu as pltpu
from jax.sharding import PartitionSpec as P

C = 128
MESH = pl.DeviceIdType.MESH
F32 = jnp.float32
BF16 = jnp.bfloat16


def zero_shift(values, step, width):
    if step == 0:
        return values
    rows = values.shape[0]
    column = lax.broadcasted_iota(jnp.int32, values.shape, 0) % width
    rolled = pltpu.roll(values, (-step) % rows, 0)
    edge = width - 1 if step > 0 else 0
    return jnp.where(column == edge, 0.0, rolled)


def kernel(
    geom, feat, cot, k1, k2, out_b, out_g, out_1, out_2,
    F, X, C_, H, G, W1, V2, W2, V1, slope, early, LT, CT, CO, PP, R0, S1, R1, E,
    wsem, hsend, hrecv, s0, r0, s1, r1, s2, r2,
):
    nz, ny, nx, width, cells_all = geom
    ntm, nrows = nz * ny, nx * 2
    oc = C // ntm
    FR, RT = feat.shape[0], feat.shape[1]
    pairs = RT // 2
    cells = FR * RT * width
    tm, rows = lax.axis_index("tm"), lax.axis_index("rows")
    z, y = tm // ny, tm % ny
    x, core = rows // 2, rows % 2
    up, down = (tm + 1) % ntm, (tm + ntm - 1) % ntm
    right, left = (rows + 1) % nrows, (rows + nrows - 1) % nrows
    partner = x * 2 + 1 - core

    loads = {}
    count = [0]

    def load(name, src, dst):
        copy = pltpu.make_async_copy(src, dst, wsem.at[count[0]])
        count[0] += 1
        copy.start()
        loads.setdefault(name, []).append(copy)

    def arrived(name):
        for copy in loads[name]:
            copy.wait()

    load("F", feat, F.at[2 : 2 + FR, 1 : 1 + RT])
    load("C", cot, C_.at[0:FR, 1 : 1 + RT])

    def load_forward(name, src, W):
        for k in range(3):
            for o in range(2):
                load(name, src.at[:, :, k], W.at[k, :, o : o + 3, :, o * C : (o + 1) * C])

    def load_backward(name, src, V):
        for k in range(3):
            for o in range(2):
                for j in range(3):
                    at = o + 2 - j
                    load(name, src.at[:, j, k], V.at[k, :, o * C : (o + 1) * C, at * C : (at + 1) * C])

    load_forward("W1", k1, W1)
    load_backward("V2", k2, V2)
    load_forward("W2", k2, W2)
    load_backward("V1", k1, V1)

    peers = [(up, right), (up, left), (down, right), (down, left)]
    peers += [(tm, (rows + o) % nrows) for o in range(1, nrows)]

    def plane_peer(dz, dy):
        return (((z + dz) % nz) * ny + (y + dy) % ny, rows)

    offsets = [(dz, dy) for dz in list(range(1, nz)) + [0] for dy in range(ny) if (dz, dy) != (0, 0)]
    peers += [plane_peer(dz, dy) for dz, dy in offsets]
    barrier = pltpu.get_barrier_semaphore()
    for peer in peers:
        pl.semaphore_signal(barrier, inc=1, device_id=peer, device_id_type=MESH)
    pl.semaphore_wait(barrier, len(peers))

    def remote(src, dst, send, recv, peer):
        copy = pltpu.make_async_remote_copy(
            src_ref=src, dst_ref=dst, send_sem=send, recv_sem=recv, device_id=peer, device_id_type=MESH
        )
        copy.start()
        return copy

    sent = []

    def send_rows(which, src, at_f, at_r, dst, before):
        own = 2 if before else 0
        frames_src, frames_dst = slice(at_f, at_f + FR), slice(own, own + FR)
        plan = [
            (slice(at_r + RT - 1, at_r + RT), slice(0, 1), (tm, right)),
            (slice(at_r, at_r + 1), slice(RT + 1, RT + 2), (tm, left)),
        ]
        copies = []
        for n, (sr, dr, peer) in enumerate(plan):
            copies.append(
                remote(src.at[frames_src, sr], dst.at[frames_dst, dr], hsend.at[which, n], hrecv.at[which, n], peer)
            )
        sent.extend(copies)
        return copies

    def send_time(which, src, at_f, at_r, dst, before):
        frames_src = slice(at_f + FR - 2, at_f + FR) if before else slice(at_f, at_f + 2)
        frames_dst = slice(0, 2) if before else slice(FR, FR + 2)
        ahead = up if before else down
        plan = [
            (slice(at_r, at_r + RT), slice(1, 1 + RT), (ahead, rows)),
            (slice(at_r + RT - 1, at_r + RT), slice(0, 1), (ahead, right)),
            (slice(at_r, at_r + 1), slice(RT + 1, RT + 2), (ahead, left)),
        ]
        copies = []
        for n, (sr, dr, peer) in enumerate(plan):
            copies.append(
                remote(
                    src.at[frames_src, sr], dst.at[frames_dst, dr], hsend.at[which, 2 + n], hrecv.at[which, 2 + n], peer
                )
            )
        sent.extend(copies)
        return copies

    def clear_rims(dst, frames, count):
        @pl.when(rows == 0)
        def _():
            dst[frames, 0] = jnp.zeros((count, width, C), BF16)

        @pl.when(rows == nrows - 1)
        def _():
            dst[frames, RT + 1] = jnp.zeros((count, width, C), BF16)

    def receive_rows(copies, dst, before):
        for copy in copies:
            copy.wait_recv()
        own = 2 if before else 0
        clear_rims(dst, slice(own, own + FR), FR)

    def receive_time(copies, dst, before):
        for copy in copies:
            copy.wait_recv()
        at = 0 if before else FR

        @pl.when(tm == (0 if before else ntm - 1))
        def _():
            dst[at : at + 2] = jnp.zeros((2, RT + 2, width, C), BF16)

        clear_rims(dst, slice(at, at + 2), 2)

    rows_f = send_rows(0, feat, 0, 0, F, True)
    rows_c = send_rows(1, cot, 0, 0, C_, False)
    time_f = send_time(0, feat, 0, 0, F, True)
    time_c = send_time(1, cot, 0, 0, C_, False)

    for W in (W1, W2):
        W[:, :, 3, :, 0:C] = jnp.zeros((3, 3, C, C), BF16)
        W[:, :, 0, :, C : 2 * C] = jnp.zeros((3, 3, C, C), BF16)
    for V in (V1, V2):
        V[:, :, 0:C, 3 * C : 4 * C] = jnp.zeros((3, 3, C, C), BF16)
        V[:, :, C : 2 * C, 0:C] = jnp.zeros((3, 3, C, C), BF16)

    def sigmoid(values):
        return 0.5 * jnp.tanh(0.5 * values) + 0.5

    def silu_into(f, r):
        feats = F[f, r].astype(F32)
        X[f, r] = (feats * sigmoid(feats)).astype(BF16)

    arrived("F")
    for f in range(2, 2 + FR):
        silu_into(f, slice(1, 1 + RT))

    half = FR // 2

    def window(field, lead, lo, count):
        parts = []
        for pair in range(pairs):
            blocks = []
            for i in lead:
                for r in range(4):
                    blocks.append(field[lo + i : lo + i + count, 2 * pair + r].reshape(count * width, C))
            parts.append(jnp.concatenate(blocks, axis=1))
        return jnp.concatenate(parts, axis=0)

    def conv_forward(field, W, lo, count):
        lhs = window(field, (0, 1, 2), lo, count)
        total = None
        for k in (1, 0, 2):
            got = jnp.dot(lhs, W[k].reshape(12 * C, 2 * C), preferred_element_type=F32)
            got = zero_shift(got, k - 1, width)
            total = got if total is None else total + got
        return total

    def conv_backward(field, V, lo, count):
        lhs = window(field, (2, 1, 0), lo, count)
        total = None
        for k in (1, 0, 2):
            rhs = jnp.concatenate([V[k, i] for i in range(3)], axis=1)
            got = lax.dot_general(lhs, rhs, (((1,), (1,)), ((), ())), preferred_element_type=F32)
            got = zero_shift(got, 1 - k, width)
            total = got if total is None else total + got
        return total

    def put(dst, at_f, at_r, values):
        deep = values.shape[0] // pairs
        count = deep // width
        for pair in range(pairs):
            for o in range(2):
                part = values[pair * deep : (pair + 1) * deep, o * C : (o + 1) * C]
                dst[at_f : at_f + count, at_r + 2 * pair + o] = part.reshape(count, width, C).astype(dst.dtype)

    def get(src, at_f, at_r, count):
        parts = []
        for pair in range(pairs):
            blocks = [src[at_f : at_f + count, at_r + 2 * pair + o].reshape(count * width, C) for o in range(2)]
            parts.append(jnp.concatenate(blocks, axis=1))
        return jnp.concatenate(parts, axis=0).astype(F32)

    def first_conv(part):
        first_out = conv_forward(X, W1, part * half, half)
        sigma = sigmoid(first_out)
        put(H, 2 + part * half, 1, first_out * sigma)
        slope[part] = sigma * (1.0 + first_out * (1.0 - sigma))

    eye = (
        lax.broadcasted_iota(jnp.int32, (C, C), 0) == lax.broadcasted_iota(jnp.int32, (C, C), 1)
    ).astype(BF16)
    spots = [(i, j) for i in range(3) for j in range(3)]

    def turned(values):
        return lax.dot_general(eye, values, (((1,), (1,)), ((), ())), preferred_element_type=F32).astype(BF16)

    groups = ((0, 4), (4, 3))

    def place_of(pair):
        group = min(pair // 8, 1)
        base, size = groups[group]
        at = pair - 8 * group
        return at // size, base + at % size

    class Taps:
        def __init__(self, g):
            self.g, self.held, self.stored, self.sent = g, [], 0, 0

        def add(self, side):
            self.held.append(side)
            if len(self.held) == 2:
                part, slot = place_of(self.stored)
                a, b = self.held
                both = jnp.concatenate([a.reshape(nz, ny, oc, C), b.reshape(nz, ny, oc, C)], axis=2)
                PP[self.g, part, :, :, slot] = both.astype(BF16)
                self.held = []
                self.stored += 1
                if self.stored in (8, 14):
                    pair_start(self.g, self.sent)
                    self.sent += 1

    def first_kernel_gradient():
        grads = G[0:FR, 1 : 1 + RT].reshape(cells, C).astype(F32)
        for k in range(3):
            LT[k * C : (k + 1) * C] = turned(zero_shift(grads, 1 - k, width).astype(BF16))
        taps = Taps(0)
        for m in range(5):
            pieces = spots[2 * m : 2 * m + 2]
            rhs = jnp.concatenate([X[i : i + FR, j : j + RT].reshape(cells, C) for i, j in pieces], axis=1)
            got = jnp.dot(LT[...], rhs, preferred_element_type=F32)
            for n in range(len(pieces)):
                for k in range(3):
                    taps.add(got[k * C : (k + 1) * C, n * C : (n + 1) * C])
        taps.add(jnp.zeros((C, C), F32))

    tall = (RT + 2) * width

    def turn_frame(f):
        CT[:, f * tall : (f + 1) * tall] = turned(C_[f].reshape(tall, C))
        CO[:, f * RT * width : (f + 1) * RT * width] = turned(C_[f, 1 : 1 + RT].reshape(RT * width, C))

    def second_kernel_gradient():
        hidden = H[2 : 2 + FR, 1 : 1 + RT].reshape(cells, C).astype(F32)
        rhs = jnp.concatenate([zero_shift(hidden, k - 1, width).astype(BF16) for k in range(3)], axis=1)

        def turned_window(a, b):
            if b == 1:
                return CO[:, a * RT * width : (a + FR) * RT * width]
            return jnp.concatenate(
                [CT[:, f * tall + b * width : f * tall + (b + RT) * width] for f in range(a, a + FR)], axis=1
            )

        taps = Taps(1)
        for i in range(3):
            lhs = jnp.concatenate([turned_window(2 - i, 2 - j) for j in range(3)], axis=0)
            got = jnp.dot(lhs, rhs, preferred_element_type=F32)
            for j in range(3):
                for k in range(3):
                    taps.add(got[j * C : (j + 1) * C, k * C : (k + 1) * C])
        taps.add(jnp.zeros((C, C), F32))

    order = [0, 1] + [nz - 1] * (nz > 2) + list(range(2, nz - 1))
    swaps, planes = {}, {0: [], 1: []}

    def cut(ref, group):
        base, size = groups[group]
        return ref.at[:, :, base : base + size]

    def pair_start(g, group):
        copy = remote(
            cut(PP.at[g, 1 - core], group), cut(R0.at[g], group), s0.at[g, group], r0.at[g, group], (tm, partner)
        )
        swaps[g, group] = copy
        sent.append(copy)

    def pair_finish(g):
        for group in range(len(groups)):
            swaps[g, group].wait_recv()
        for dz in order:
            at = (z + dz) % nz
            S1[g, at] = (PP[g, core, at].astype(F32) + R0[g, at].astype(F32)).astype(BF16)
            for dy in range(ny):
                if (dz, dy) == (0, 0):
                    continue
                e = dz * ny + dy - 1
                source = S1.at[g, at, (y + dy) % ny]
                copy = remote(source, R1.at[g, e], s1.at[g, e], r1.at[g, e], plane_peer(dz, dy))
                planes[g].append(copy)
                sent.append(copy)

    last = []
    scale = 1.0 / math.sqrt(cells_all)

    def plane_finish(g):
        for copy in planes[g]:
            copy.wait_recv()
        total = S1[g, z, y].astype(F32)
        for e in range(ntm - 1):
            total = total + R1[g, e].astype(F32)
        E[g, core, x] = total.astype(BF16)
        more = [
            remote(
                E.at[g, core, x], E.at[g, core, x], s2.at[g, o - 1], r2.at[g, o - 1], (tm, (rows + o) % nrows)
            )
            for o in range(1, nrows)
        ]
        last.extend(more)

    def give(g, out):
        for o in range(1, nrows):
            giver = (rows + nrows - o) % nrows
            block = E.at[g, giver % 2, giver // 2]
            pltpu.make_async_remote_copy(
                src_ref=block, dst_ref=block, send_sem=s2.at[g, o - 1], recv_sem=r2.at[g, o - 1],
                device_id=(tm, (rows + o) % nrows), device_id_type=MESH,
            ).wait_recv()
        for pair in range(14):
            part, slot = place_of(pair)
            values = E[g, part, 0, slot].astype(F32)
            for at in range(1, nx):
                values = values + E[g, part, at, slot].astype(F32)
            values = values * scale
            out[2 * pair] = values[0:oc]
            if pair < 13:
                out[2 * pair + 1] = values[oc : 2 * oc]

    receive_rows(rows_f, F, True)
    for f in range(2, 2 + FR):
        silu_into(f, slice(0, 1))
        silu_into(f, slice(RT + 1, RT + 2))
    arrived("W1")
    first_conv(1)
    time_h = send_time(2, H, 2, 1, H, True)
    arrived("C")
    receive_rows(rows_c, C_, False)
    arrived("V2")
    early[...] = conv_backward(C_, V2, 0, half)
    for f in range(FR):
        turn_frame(f)

    receive_time(time_f, F, True)
    for f in range(2):
        silu_into(f, slice(0, RT + 2))
    first_conv(0)
    rows_h = send_rows(2, H, 2, 1, H, True)
    put(G, 0, 1, early[...] * slope[0])
    time_g = send_time(3, G, 0, 1, G, False)

    receive_time(time_c, C_, False)
    for f in range(FR, FR + 2):
        turn_frame(f)
    second_kernel_gradient()
    put(G, half, 1, conv_backward(C_, V2, half, half) * slope[1])
    rows_g = send_rows(3, G, 0, 1, G, False)
    pair_finish(1)
    first_kernel_gradient()
    pair_finish(0)

    receive_rows(rows_h, H, True)
    receive_time(time_h, H, True)
    arrived("W2")
    put(out_b, 0, 0, get(F, 2, 1, FR) + conv_forward(H, W2, 0, FR))

    plane_finish(1)

    receive_rows(rows_g, G, False)
    receive_time(time_g, G, False)
    arrived("V1")
    feats = get(F, 2, 1, FR)
    sigma = sigmoid(feats)
    turn = sigma * (1.0 + feats * (1.0 - sigma))
    put(out_g, 0, 0, get(C_, 0, 1, FR) + conv_backward(G, V1, 0, FR) * turn)

    plane_finish(0)
    for copy in sent:
        copy.wait_send()
    give(1, out_2)
    give(0, out_1)
    for copy in last:
        copy.wait_send()


def hand_out(a, b, c, d, out_a, out_b, out_c, out_d, sems):
    pairs = ((a, out_a), (b, out_b), (c, out_c), (d, out_d))
    copies = [pltpu.make_async_copy(src, dst, sems.at[n]) for n, (src, dst) in enumerate(pairs)]
    for copy in copies:
        copy.start()
    for copy in copies:
        copy.wait()


def build(geom, features, cotangent, first_kernel, second_kernel):
    nz, ny, nx, width, cells_all = geom
    FR, RT = features.shape[0], features.shape[1]
    ntm = nz * ny
    oc = C // ntm
    tall = 2 * oc
    cells = FR * RT * width
    pad = pltpu.VMEM((FR + 2, RT + 2, width, C), BF16)
    forward = pltpu.VMEM((3, 3, 4, C, 2 * C), BF16)
    backward = pltpu.VMEM((3, 3, 2 * C, 4 * C), BF16)
    block = (7, tall, C)
    scratch = [
        pad, pad, pad, pad, pad,
        forward, backward, forward, backward,
        pltpu.VMEM((2, cells // 4, 2 * C), F32),
        pltpu.VMEM((cells // 4, 2 * C), F32),
        pltpu.VMEM((3 * C, cells), BF16),
        pltpu.VMEM((C, (FR + 2) * (RT + 2) * width), BF16),
        pltpu.VMEM((C, (FR + 2) * RT * width), BF16),
        pltpu.VMEM((2, 2, nz, ny) + block, BF16),
        pltpu.VMEM((2, nz, ny) + block, BF16),
        pltpu.VMEM((2, nz, ny) + block, BF16),
        pltpu.VMEM((2, ntm - 1) + block, BF16),
        pltpu.VMEM((2, 2, nx) + block, BF16),
        pltpu.SemaphoreType.DMA((50,)),
        pltpu.SemaphoreType.DMA((4, 5)),
        pltpu.SemaphoreType.DMA((4, 5)),
        pltpu.SemaphoreType.DMA((2, 3)),
        pltpu.SemaphoreType.DMA((2, 3)),
        pltpu.SemaphoreType.DMA((2, ntm - 1)),
        pltpu.SemaphoreType.DMA((2, ntm - 1)),
        pltpu.SemaphoreType.DMA((2, 2 * nx - 1)),
        pltpu.SemaphoreType.DMA((2, 2 * nx - 1)),
    ]
    anywhere = pl.BlockSpec(memory_space=pl.ANY)
    features, cotangent, first_kernel, second_kernel = [
        pltpu.with_memory_space_constraint(value, pltpu.HBM)
        for value in (features, cotangent, first_kernel, second_kernel)
    ]
    field = jax.ShapeDtypeStruct(features.shape, BF16)
    grads = jax.ShapeDtypeStruct((27, oc, C), F32)
    block_out, grad_input, g1, g2 = pl.pallas_call(
        functools.partial(kernel, geom),
        out_shape=(field, field, grads, grads),
        in_specs=[anywhere] * 4,
        out_specs=(pl.BlockSpec(memory_space=pltpu.VMEM),) * 4,
        scratch_shapes=scratch,
        compiler_params=pltpu.CompilerParams(
            collective_id=0, has_side_effects=True, vmem_limit_bytes=48 * 1024 * 1024
        ),
    )(features, cotangent, first_kernel, second_kernel)

    block_out, grad_input, g1, g2 = pl.pallas_call(
        hand_out,
        out_shape=(field, field, grads, grads),
        in_specs=[anywhere] * 4,
        out_specs=(anywhere,) * 4,
        scratch_shapes=[pltpu.SemaphoreType.DMA((4,))],
        compiler_params=pltpu.CompilerParams(vmem_limit_bytes=8 * 1024 * 1024),
    )(block_out, grad_input, g1, g2)

    def place(values):
        return jnp.transpose(values.reshape(3, 3, 3, oc, C), (0, 1, 2, 4, 3))

    return block_out, grad_input, place(g1), place(g2)


def solution(mesh, sides=(4, 4, 4)):
    nz, ny, nx = sides

    def on_device(features, cotangent, first_kernel, second_kernel):
        width = features.shape[2]
        cells_all = features.shape[0] * features.shape[1] * width * nz * ny * nx * 2
        geom = (nz, ny, nx, width, cells_all)
        return build(geom, features, cotangent, first_kernel, second_kernel)

    return jax.shard_map(
        on_device,
        mesh=mesh,
        in_specs=(P("tm", "rows", None, None), P("tm", "rows", None, None), P(), P()),
        out_specs=(
            P("tm", "rows", None, None),
            P("tm", "rows", None, None),
            P(None, None, None, None, "tm"),
            P(None, None, None, None, "tm"),
        ),
        check_vma=False,
    )
```

```python
import functools
import math

import jax
import jax.numpy as jnp
from jax import lax
from jax.experimental import pallas as pl
from jax.experimental.pallas import tpu as pltpu
from jax.sharding import PartitionSpec as P

C = 128
MESH = pl.DeviceIdType.MESH
F32 = jnp.float32
BF16 = jnp.bfloat16


def zero_shift(values, step, width):
    if step == 0:
        return values
    rows = values.shape[0]
    column = lax.broadcasted_iota(jnp.int32, values.shape, 0) % width
    rolled = pltpu.roll(values, (-step) % rows, 0)
    edge = width - 1 if step > 0 else 0
    return jnp.where(column == edge, 0.0, rolled)


def kernel(
    geom, feat, cot, k1, k2, out_b, out_g, out_1, out_2,
    F, X, C_, H, G, W1, V2, W2, V1, slope, early, LT, CT, CO, PP, R0, S1, S2, A1, A2, E,
    wsem, hsend, hrecv, s0, r0, s1, r1, s2, r2, s3, r3,
):
    nz, ny, nx, width, cells_all = geom
    ntm, nrows = nz * ny, nx * 2
    oc = C // ntm
    FR, RT = feat.shape[0], feat.shape[1]
    pairs = RT // 2
    cells = FR * RT * width
    tm, rows = lax.axis_index("tm"), lax.axis_index("rows")
    z, y = tm // ny, tm % ny
    x, core = rows // 2, rows % 2
    up, down = (tm + 1) % ntm, (tm + ntm - 1) % ntm
    right, left = (rows + 1) % nrows, (rows + nrows - 1) % nrows
    partner = x * 2 + 1 - core

    loads = {}
    count = [0]

    def load(name, src, dst):
        copy = pltpu.make_async_copy(src, dst, wsem.at[count[0]])
        count[0] += 1
        copy.start()
        loads.setdefault(name, []).append(copy)

    def arrived(name):
        for copy in loads[name]:
            copy.wait()

    load("F", feat, F.at[2 : 2 + FR, 1 : 1 + RT])
    load("C", cot, C_.at[0:FR, 1 : 1 + RT])

    def load_forward(name, src, W):
        for k in range(3):
            for o in range(2):
                load(name, src.at[:, :, k], W.at[k, :, o : o + 3, :, o * C : (o + 1) * C])

    def load_backward(name, src, V):
        for k in range(3):
            for o in range(2):
                for j in range(3):
                    at = o + 2 - j
                    load(name, src.at[:, j, k], V.at[k, :, o * C : (o + 1) * C, at * C : (at + 1) * C])

    load_forward("W1", k1, W1)
    load_backward("V2", k2, V2)
    load_forward("W2", k2, W2)
    load_backward("V1", k1, V1)

    peers = [(up, rows), (up, right), (up, left), (down, rows), (down, right), (down, left)]
    peers += [(tm, (rows + o) % nrows) for o in range(1, nrows)]

    def plane_peer(dz, dy):
        return (((z + dz) % nz) * ny + (y + dy) % ny, rows)

    peers += [plane_peer(0, dy) for dy in range(1, ny)] + [plane_peer(dz, 0) for dz in range(1, nz)]
    barrier = pltpu.get_barrier_semaphore()
    for peer in peers:
        pl.semaphore_signal(barrier, inc=1, device_id=peer, device_id_type=MESH)
    pl.semaphore_wait(barrier, len(peers))

    def remote(src, dst, send, recv, peer):
        copy = pltpu.make_async_remote_copy(
            src_ref=src, dst_ref=dst, send_sem=send, recv_sem=recv, device_id=peer, device_id_type=MESH
        )
        copy.start()
        return copy

    sent = []

    def send_rows(which, src, at_f, at_r, dst, before):
        own = 2 if before else 0
        frames_src, frames_dst = slice(at_f, at_f + FR), slice(own, own + FR)
        plan = [
            (slice(at_r + RT - 1, at_r + RT), slice(0, 1), (tm, right)),
            (slice(at_r, at_r + 1), slice(RT + 1, RT + 2), (tm, left)),
        ]
        copies = []
        for n, (sr, dr, peer) in enumerate(plan):
            copies.append(
                remote(src.at[frames_src, sr], dst.at[frames_dst, dr], hsend.at[which, n], hrecv.at[which, n], peer)
            )
        sent.extend(copies)
        return copies

    def send_time(which, src, at_f, at_r, dst, before):
        frames_src = slice(at_f + FR - 2, at_f + FR) if before else slice(at_f, at_f + 2)
        frames_dst = slice(0, 2) if before else slice(FR, FR + 2)
        ahead = up if before else down
        plan = [
            (slice(at_r, at_r + RT), slice(1, 1 + RT), (ahead, rows)),
            (slice(at_r + RT - 1, at_r + RT), slice(0, 1), (ahead, right)),
            (slice(at_r, at_r + 1), slice(RT + 1, RT + 2), (ahead, left)),
        ]
        copies = []
        for n, (sr, dr, peer) in enumerate(plan):
            copies.append(
                remote(
                    src.at[frames_src, sr], dst.at[frames_dst, dr], hsend.at[which, 2 + n], hrecv.at[which, 2 + n], peer
                )
            )
        sent.extend(copies)
        return copies

    def clear_rims(dst, frames, count):
        @pl.when(rows == 0)
        def _():
            dst[frames, 0] = jnp.zeros((count, width, C), BF16)

        @pl.when(rows == nrows - 1)
        def _():
            dst[frames, RT + 1] = jnp.zeros((count, width, C), BF16)

    def receive_rows(copies, dst, before):
        for copy in copies:
            copy.wait_recv()
        own = 2 if before else 0
        clear_rims(dst, slice(own, own + FR), FR)

    def receive_time(copies, dst, before):
        for copy in copies:
            copy.wait_recv()
        at = 0 if before else FR

        @pl.when(tm == (0 if before else ntm - 1))
        def _():
            dst[at : at + 2] = jnp.zeros((2, RT + 2, width, C), BF16)

        clear_rims(dst, slice(at, at + 2), 2)

    rows_f = send_rows(0, feat, 0, 0, F, True)
    rows_c = send_rows(1, cot, 0, 0, C_, False)
    time_f = send_time(0, feat, 0, 0, F, True)
    time_c = send_time(1, cot, 0, 0, C_, False)

    for W in (W1, W2):
        W[:, :, 3, :, 0:C] = jnp.zeros((3, 3, C, C), BF16)
        W[:, :, 0, :, C : 2 * C] = jnp.zeros((3, 3, C, C), BF16)
    for V in (V1, V2):
        V[:, :, 0:C, 3 * C : 4 * C] = jnp.zeros((3, 3, C, C), BF16)
        V[:, :, C : 2 * C, 0:C] = jnp.zeros((3, 3, C, C), BF16)

    def sigmoid(values):
        return 0.5 * jnp.tanh(0.5 * values) + 0.5

    def silu_into(f, r):
        feats = F[f, r].astype(F32)
        X[f, r] = (feats * sigmoid(feats)).astype(BF16)

    arrived("F")
    for f in range(2, 2 + FR):
        silu_into(f, slice(1, 1 + RT))

    half = FR // 2

    def window(field, lead, lo, count):
        parts = []
        for pair in range(pairs):
            blocks = []
            for i in lead:
                for r in range(4):
                    blocks.append(field[lo + i : lo + i + count, 2 * pair + r].reshape(count * width, C))
            parts.append(jnp.concatenate(blocks, axis=1))
        return jnp.concatenate(parts, axis=0)

    def conv_forward(field, W, lo, count, taps=(0, 1, 2)):
        lhs = window(field, taps, lo, count)
        deep = len(taps) * 4 * C
        total = None
        for k in (1, 0, 2):
            rhs = W[k, taps[0] : taps[-1] + 1].reshape(deep, 2 * C)
            got = jnp.dot(lhs, rhs, preferred_element_type=F32)
            got = zero_shift(got, k - 1, width)
            total = got if total is None else total + got
        return total

    def conv_backward(field, V, lo, count, taps=(0, 1, 2)):
        lhs = window(field, [2 - i for i in taps], lo, count)
        total = None
        for k in (1, 0, 2):
            rhs = jnp.concatenate([V[k, i] for i in taps], axis=1)
            got = lax.dot_general(lhs, rhs, (((1,), (1,)), ((), ())), preferred_element_type=F32)
            got = zero_shift(got, 1 - k, width)
            total = got if total is None else total + got
        return total

    def put(dst, at_f, at_r, values):
        deep = values.shape[0] // pairs
        count = deep // width
        for pair in range(pairs):
            for o in range(2):
                part = values[pair * deep : (pair + 1) * deep, o * C : (o + 1) * C]
                dst[at_f : at_f + count, at_r + 2 * pair + o] = part.reshape(count, width, C).astype(dst.dtype)

    def get(src, at_f, at_r, count):
        parts = []
        for pair in range(pairs):
            blocks = [src[at_f : at_f + count, at_r + 2 * pair + o].reshape(count * width, C) for o in range(2)]
            parts.append(jnp.concatenate(blocks, axis=1))
        return jnp.concatenate(parts, axis=0).astype(F32)

    def first_conv(part):
        if part == 0:
            first_out = conv_forward(X, W1, 0, half, (0, 1)) + early[1]
        else:
            first_out = conv_forward(X, W1, half, half)
        sigma = sigmoid(first_out)
        put(H, 2 + part * half, 1, first_out * sigma)
        slope[part] = sigma * (1.0 + first_out * (1.0 - sigma))

    eye = (
        lax.broadcasted_iota(jnp.int32, (C, C), 0) == lax.broadcasted_iota(jnp.int32, (C, C), 1)
    ).astype(BF16)
    spots = [(i, j) for i in range(3) for j in range(3)]

    def turned(values):
        return lax.dot_general(eye, values, (((1,), (1,)), ((), ())), preferred_element_type=F32).astype(BF16)

    groups = ((0, 4), (4, 3))

    def place_of(pair):
        group = min(pair // 8, 1)
        base, size = groups[group]
        at = pair - 8 * group
        return at // size, base + at % size

    class Taps:
        def __init__(self, g):
            self.g, self.held, self.stored, self.sent = g, [], 0, 0

        def add(self, side):
            self.held.append(side)
            if len(self.held) == 2:
                part, slot = place_of(self.stored)
                a, b = self.held
                both = jnp.concatenate([a.reshape(nz, ny, oc, C), b.reshape(nz, ny, oc, C)], axis=2)
                if part == 1:
                    both = jnp.transpose(both, (1, 0, 2, 3))
                PP[self.g, part, :, :, slot] = both.astype(BF16)
                self.held = []
                self.stored += 1
                if self.stored in (8, 14):
                    pair_start(self.g, self.sent)
                    self.sent += 1

    def first_kernel_gradient():
        grads = G[0:FR, 1 : 1 + RT].reshape(cells, C).astype(F32)
        for k in range(3):
            LT[k * C : (k + 1) * C] = turned(zero_shift(grads, 1 - k, width).astype(BF16))
        taps = Taps(0)
        for m in range(5):
            pieces = spots[2 * m : 2 * m + 2]
            rhs = jnp.concatenate([X[i : i + FR, j : j + RT].reshape(cells, C) for i, j in pieces], axis=1)
            got = jnp.dot(LT[...], rhs, preferred_element_type=F32)
            for n in range(len(pieces)):
                for k in range(3):
                    taps.add(got[k * C : (k + 1) * C, n * C : (n + 1) * C])
        taps.add(jnp.zeros((C, C), F32))

    tall = (RT + 2) * width

    def turn_frame(f):
        CT[:, f * tall : (f + 1) * tall] = turned(C_[f].reshape(tall, C))
        CO[:, f * RT * width : (f + 1) * RT * width] = turned(C_[f, 1 : 1 + RT].reshape(RT * width, C))

    def second_kernel_gradient():
        hidden = H[2 : 2 + FR, 1 : 1 + RT].reshape(cells, C).astype(F32)
        rhs = jnp.concatenate([zero_shift(hidden, k - 1, width).astype(BF16) for k in range(3)], axis=1)

        def turned_window(a, b):
            if b == 1:
                return CO[:, a * RT * width : (a + FR) * RT * width]
            return jnp.concatenate(
                [CT[:, f * tall + b * width : f * tall + (b + RT) * width] for f in range(a, a + FR)], axis=1
            )

        taps = Taps(1)
        for i in range(3):
            lhs = jnp.concatenate([turned_window(2 - i, 2 - j) for j in range(3)], axis=0)
            got = jnp.dot(lhs, rhs, preferred_element_type=F32)
            for j in range(3):
                for k in range(3):
                    taps.add(got[j * C : (j + 1) * C, k * C : (k + 1) * C])
        taps.add(jnp.zeros((C, C), F32))

    swaps, axes = {}, {0: [], 1: []}

    def cut(ref, group):
        base, size = groups[group]
        return ref.at[:, :, base : base + size]

    def pair_start(g, group):
        copy = remote(
            cut(PP.at[g, 1 - core], group), cut(R0.at[g], group), s0.at[g, group], r0.at[g, group], (tm, partner)
        )
        swaps[g, group] = copy
        sent.append(copy)

    first, second = (1 - core) * z + core * y, (1 - core) * y + core * z

    def axis_peer(d, turn):
        along_z = (1 - core) * (1 - turn) + core * turn
        return (((z + d * along_z) % nz) * ny + (y + d * (1 - along_z)) % ny, rows)

    def axis_start(g):
        for group in range(len(groups)):
            swaps[g, group].wait_recv()
        for d in range(nz):
            at = (first + nz - d) % nz
            S1[g, at] = (PP[g, core, at].astype(F32) + R0[g, at].astype(F32)).astype(BF16)
            if d:
                copy = remote(S1.at[g, at], A1.at[g, d - 1], s1.at[g, d - 1], r1.at[g, d - 1], axis_peer(nz - d, 0))
                axes[g].append(copy)
                sent.append(copy)

    def axis_turn(g):
        for copy in axes[g]:
            copy.wait_recv()
        total = S1[g, first].astype(F32)
        for d in range(1, nz):
            total = total + A1[g, d - 1].astype(F32)
        S2[g] = total.astype(BF16)
        axes[g] = []
        for d in range(1, nz):
            at = (second + d) % nz
            copy = remote(S2.at[g, at], A2.at[g, d - 1], s3.at[g, d - 1], r3.at[g, d - 1], axis_peer(d, 1))
            axes[g].append(copy)
            sent.append(copy)

    last = []
    scale = 1.0 / math.sqrt(cells_all)

    def axes_finish(g):
        for copy in axes[g]:
            copy.wait_recv()
        total = S2[g, second].astype(F32)
        for d in range(1, nz):
            total = total + A2[g, d - 1].astype(F32)
        E[g, core, x] = total.astype(BF16)
        more = [
            remote(
                E.at[g, core, x], E.at[g, core, x], s2.at[g, o - 1], r2.at[g, o - 1], (tm, (rows + o) % nrows)
            )
            for o in range(1, nrows)
        ]
        last.extend(more)

    def give(g, out):
        for o in range(1, nrows):
            giver = (rows + nrows - o) % nrows
            block = E.at[g, giver % 2, giver // 2]
            pltpu.make_async_remote_copy(
                src_ref=block, dst_ref=block, send_sem=s2.at[g, o - 1], recv_sem=r2.at[g, o - 1],
                device_id=(tm, (rows + o) % nrows), device_id_type=MESH,
            ).wait_recv()
        for pair in range(14):
            part, slot = place_of(pair)
            values = E[g, part, 0, slot].astype(F32)
            for at in range(1, nx):
                values = values + E[g, part, at, slot].astype(F32)
            values = values * scale
            out[2 * pair] = values[0:oc]
            if pair < 13:
                out[2 * pair + 1] = values[oc : 2 * oc]

    receive_rows(rows_f, F, True)
    for f in range(2, 2 + FR):
        silu_into(f, slice(0, 1))
        silu_into(f, slice(RT + 1, RT + 2))
    arrived("W1")
    first_conv(1)
    time_h = send_time(2, H, 2, 1, H, True)
    arrived("C")
    receive_rows(rows_c, C_, False)
    arrived("V2")
    early[0] = conv_backward(C_, V2, 0, half)
    early[1] = conv_forward(X, W1, 0, half, (2,))
    early[2] = conv_backward(C_, V2, half, half, (2,))
    for f in range(FR):
        turn_frame(f)

    receive_time(time_f, F, True)
    for f in range(2):
        silu_into(f, slice(0, RT + 2))
    first_conv(0)
    rows_h = send_rows(2, H, 2, 1, H, True)
    put(G, 0, 1, early[0] * slope[0])
    time_g = send_time(3, G, 0, 1, G, False)

    receive_time(time_c, C_, False)
    for f in range(FR, FR + 2):
        turn_frame(f)
    second_kernel_gradient()
    put(G, half, 1, (conv_backward(C_, V2, half, half, (0, 1)) + early[2]) * slope[1])
    rows_g = send_rows(3, G, 0, 1, G, False)
    axis_start(1)
    first_kernel_gradient()
    axis_start(0)
    axis_turn(1)
    receive_rows(rows_h, H, True)
    receive_time(time_h, H, True)
    arrived("W2")
    put(out_b, 0, 0, get(F, 2, 1, FR) + conv_forward(H, W2, 0, FR))

    axis_turn(0)
    receive_rows(rows_g, G, False)
    receive_time(time_g, G, False)
    arrived("V1")
    feats = get(F, 2, 1, FR)
    sigma = sigmoid(feats)
    turn = sigma * (1.0 + feats * (1.0 - sigma))
    put(out_g, 0, 0, get(C_, 0, 1, FR) + conv_backward(G, V1, 0, FR) * turn)

    axes_finish(1)
    axes_finish(0)
    for copy in sent:
        copy.wait_send()
    give(1, out_2)
    give(0, out_1)
    for copy in last:
        copy.wait_send()


def hand_out(a, b, c, d, out_a, out_b, out_c, out_d, sems):
    pairs = ((a, out_a), (b, out_b), (c, out_c), (d, out_d))
    copies = [pltpu.make_async_copy(src, dst, sems.at[n]) for n, (src, dst) in enumerate(pairs)]
    for copy in copies:
        copy.start()
    for copy in copies:
        copy.wait()


def build(geom, features, cotangent, first_kernel, second_kernel):
    nz, ny, nx, width, cells_all = geom
    FR, RT = features.shape[0], features.shape[1]
    ntm = nz * ny
    oc = C // ntm
    tall = 2 * oc
    cells = FR * RT * width
    pad = pltpu.VMEM((FR + 2, RT + 2, width, C), BF16)
    forward = pltpu.VMEM((3, 3, 4, C, 2 * C), BF16)
    backward = pltpu.VMEM((3, 3, 2 * C, 4 * C), BF16)
    block = (7, tall, C)
    scratch = [
        pad, pad, pad, pad, pad,
        forward, backward, forward, backward,
        pltpu.VMEM((2, cells // 4, 2 * C), F32),
        pltpu.VMEM((3, cells // 4, 2 * C), F32),
        pltpu.VMEM((3 * C, cells), BF16),
        pltpu.VMEM((C, (FR + 2) * (RT + 2) * width), BF16),
        pltpu.VMEM((C, (FR + 2) * RT * width), BF16),
        pltpu.VMEM((2, 2, nz, ny) + block, BF16),
        pltpu.VMEM((2, nz, ny) + block, BF16),
        pltpu.VMEM((2, nz, ny) + block, BF16),
        pltpu.VMEM((2, ny) + block, BF16),
        pltpu.VMEM((2, nz - 1, ny) + block, BF16),
        pltpu.VMEM((2, nz - 1) + block, BF16),
        pltpu.VMEM((2, 2, nx) + block, BF16),
        pltpu.SemaphoreType.DMA((50,)),
        pltpu.SemaphoreType.DMA((4, 5)),
        pltpu.SemaphoreType.DMA((4, 5)),
        pltpu.SemaphoreType.DMA((2, 3)),
        pltpu.SemaphoreType.DMA((2, 3)),
        pltpu.SemaphoreType.DMA((2, nz - 1)),
        pltpu.SemaphoreType.DMA((2, nz - 1)),
        pltpu.SemaphoreType.DMA((2, 2 * nx - 1)),
        pltpu.SemaphoreType.DMA((2, 2 * nx - 1)),
        pltpu.SemaphoreType.DMA((2, nz - 1)),
        pltpu.SemaphoreType.DMA((2, nz - 1)),
    ]
    anywhere = pl.BlockSpec(memory_space=pl.ANY)
    features, cotangent, first_kernel, second_kernel = [
        pltpu.with_memory_space_constraint(value, pltpu.HBM)
        for value in (features, cotangent, first_kernel, second_kernel)
    ]
    field = jax.ShapeDtypeStruct(features.shape, BF16)
    grads = jax.ShapeDtypeStruct((27, oc, C), F32)
    block_out, grad_input, g1, g2 = pl.pallas_call(
        functools.partial(kernel, geom),
        out_shape=(field, field, grads, grads),
        in_specs=[anywhere] * 4,
        out_specs=(pl.BlockSpec(memory_space=pltpu.VMEM),) * 4,
        scratch_shapes=scratch,
        compiler_params=pltpu.CompilerParams(
            collective_id=0, has_side_effects=True, vmem_limit_bytes=48 * 1024 * 1024
        ),
    )(features, cotangent, first_kernel, second_kernel)

    block_out, grad_input, g1, g2 = pl.pallas_call(
        hand_out,
        out_shape=(field, field, grads, grads),
        in_specs=[anywhere] * 4,
        out_specs=(anywhere,) * 4,
        scratch_shapes=[pltpu.SemaphoreType.DMA((4,))],
        compiler_params=pltpu.CompilerParams(vmem_limit_bytes=8 * 1024 * 1024),
    )(block_out, grad_input, g1, g2)

    def place(values):
        return jnp.transpose(values.reshape(3, 3, 3, oc, C), (0, 1, 2, 4, 3))

    return block_out, grad_input, place(g1), place(g2)


def solution(mesh, sides=(4, 4, 4)):
    nz, ny, nx = sides

    def on_device(features, cotangent, first_kernel, second_kernel):
        width = features.shape[2]
        cells_all = features.shape[0] * features.shape[1] * width * nz * ny * nx * 2
        geom = (nz, ny, nx, width, cells_all)
        return build(geom, features, cotangent, first_kernel, second_kernel)

    return jax.shard_map(
        on_device,
        mesh=mesh,
        in_specs=(P("tm", "rows", None, None), P("tm", "rows", None, None), P(), P()),
        out_specs=(
            P("tm", "rows", None, None),
            P("tm", "rows", None, None),
            P(None, None, None, None, "tm"),
            P(None, None, None, None, "tm"),
        ),
        check_vma=False,
    )
```

```python
import functools
import math

import jax
import jax.numpy as jnp
from jax import lax
from jax.experimental import pallas as pl
from jax.experimental.pallas import tpu as pltpu
from jax.sharding import PartitionSpec as P

C = 128
MESH = pl.DeviceIdType.MESH
F32 = jnp.float32
BF16 = jnp.bfloat16


def zero_shift(values, step, width):
    if step == 0:
        return values
    rows = values.shape[0]
    column = lax.broadcasted_iota(jnp.int32, values.shape, 0) % width
    rolled = pltpu.roll(values, (-step) % rows, 0)
    edge = width - 1 if step > 0 else 0
    return jnp.where(column == edge, 0.0, rolled)


def kernel(
    geom, feat, cot, k1, k2, out_b, out_g, out_1, out_2,
    F, X, C_, H, G, W1, V2, W2, V1, slope, early, LT, CT, CO, PP, R0, S1, S2, A1, A2, E,
    wsem, hsend, hrecv, s0, r0, s1, r1, s2, r2, s3, r3,
):
    nz, ny, nx, width, cells_all = geom
    ntm, nrows = nz * ny, nx * 2
    oc = C // ntm
    FR, RT = feat.shape[0], feat.shape[1]
    pairs = RT // 2
    cells = FR * RT * width
    tm, rows = lax.axis_index("tm"), lax.axis_index("rows")
    z, y = tm // ny, tm % ny
    x, core = rows // 2, rows % 2
    up, down = (tm + 1) % ntm, (tm + ntm - 1) % ntm
    right, left = (rows + 1) % nrows, (rows + nrows - 1) % nrows
    partner = x * 2 + 1 - core

    loads = {}
    count = [0]

    def load(name, src, dst):
        copy = pltpu.make_async_copy(src, dst, wsem.at[count[0]])
        count[0] += 1
        copy.start()
        loads.setdefault(name, []).append(copy)

    def arrived(name):
        for copy in loads[name]:
            copy.wait()

    load("F", feat, F.at[2 : 2 + FR, 1 : 1 + RT])
    load("C", cot, C_.at[0:FR, 1 : 1 + RT])

    def load_forward(name, src, W):
        for k in range(3):
            for o in range(2):
                load(name, src.at[:, :, k], W.at[k, :, o : o + 3, :, o * C : (o + 1) * C])

    def load_backward(name, src, V):
        for k in range(3):
            for o in range(2):
                for j in range(3):
                    at = o + 2 - j
                    load(name, src.at[:, j, k], V.at[k, :, o * C : (o + 1) * C, at * C : (at + 1) * C])

    load_forward("W1", k1, W1)
    load_backward("V2", k2, V2)
    load_forward("W2", k2, W2)
    load_backward("V1", k1, V1)

    peers = [(up, rows), (up, right), (up, left), (down, rows), (down, right), (down, left)]
    peers += [(tm, (rows + o) % nrows) for o in range(1, nrows)]

    def plane_peer(dz, dy):
        return (((z + dz) % nz) * ny + (y + dy) % ny, rows)

    peers += [plane_peer(0, dy) for dy in range(1, ny)] + [plane_peer(dz, 0) for dz in range(1, nz)]
    barrier = pltpu.get_barrier_semaphore()
    for peer in peers:
        pl.semaphore_signal(barrier, inc=1, device_id=peer, device_id_type=MESH)
    pl.semaphore_wait(barrier, len(peers))

    def remote(src, dst, send, recv, peer):
        copy = pltpu.make_async_remote_copy(
            src_ref=src, dst_ref=dst, send_sem=send, recv_sem=recv, device_id=peer, device_id_type=MESH
        )
        copy.start()
        return copy

    sent = []

    def send_rows(which, src, at_f, at_r, dst, before):
        own = 2 if before else 0
        frames_src, frames_dst = slice(at_f, at_f + FR), slice(own, own + FR)
        plan = [
            (slice(at_r + RT - 1, at_r + RT), slice(0, 1), (tm, right)),
            (slice(at_r, at_r + 1), slice(RT + 1, RT + 2), (tm, left)),
        ]
        copies = []
        for n, (sr, dr, peer) in enumerate(plan):
            copies.append(
                remote(src.at[frames_src, sr], dst.at[frames_dst, dr], hsend.at[which, n], hrecv.at[which, n], peer)
            )
        sent.extend(copies)
        return copies

    def send_time(which, src, at_f, at_r, dst, before):
        frames_src = slice(at_f + FR - 2, at_f + FR) if before else slice(at_f, at_f + 2)
        frames_dst = slice(0, 2) if before else slice(FR, FR + 2)
        ahead = up if before else down
        plan = [
            (slice(at_r, at_r + RT), slice(1, 1 + RT), (ahead, rows)),
            (slice(at_r + RT - 1, at_r + RT), slice(0, 1), (ahead, right)),
            (slice(at_r, at_r + 1), slice(RT + 1, RT + 2), (ahead, left)),
        ]
        copies = []
        for n, (sr, dr, peer) in enumerate(plan):
            copies.append(
                remote(
                    src.at[frames_src, sr], dst.at[frames_dst, dr], hsend.at[which, 2 + n], hrecv.at[which, 2 + n], peer
                )
            )
        sent.extend(copies)
        return copies

    def clear_rims(dst, frames, count):
        @pl.when(rows == 0)
        def _():
            dst[frames, 0] = jnp.zeros((count, width, C), BF16)

        @pl.when(rows == nrows - 1)
        def _():
            dst[frames, RT + 1] = jnp.zeros((count, width, C), BF16)

    def receive_rows(copies, dst, before):
        for copy in copies:
            copy.wait_recv()
        own = 2 if before else 0
        clear_rims(dst, slice(own, own + FR), FR)

    def receive_time(copies, dst, before):
        for copy in copies:
            copy.wait_recv()
        at = 0 if before else FR

        @pl.when(tm == (0 if before else ntm - 1))
        def _():
            dst[at : at + 2] = jnp.zeros((2, RT + 2, width, C), BF16)

        clear_rims(dst, slice(at, at + 2), 2)

    rows_f = send_rows(0, feat, 0, 0, F, True)
    rows_c = send_rows(1, cot, 0, 0, C_, False)
    time_f = send_time(0, feat, 0, 0, F, True)
    time_c = send_time(1, cot, 0, 0, C_, False)

    for W in (W1, W2):
        W[:, :, 3, :, 0:C] = jnp.zeros((3, 3, C, C), BF16)
        W[:, :, 0, :, C : 2 * C] = jnp.zeros((3, 3, C, C), BF16)
    for V in (V1, V2):
        V[:, :, 0:C, 3 * C : 4 * C] = jnp.zeros((3, 3, C, C), BF16)
        V[:, :, C : 2 * C, 0:C] = jnp.zeros((3, 3, C, C), BF16)

    def sigmoid(values):
        return 0.5 * jnp.tanh(0.5 * values) + 0.5

    def silu_into(f, r):
        feats = F[f, r].astype(F32)
        X[f, r] = (feats * sigmoid(feats)).astype(BF16)

    arrived("F")
    for f in range(2, 2 + FR):
        silu_into(f, slice(1, 1 + RT))

    half = FR // 2

    def window(field, lead, lo, count):
        parts = []
        for pair in range(pairs):
            blocks = []
            for i in lead:
                for r in range(4):
                    blocks.append(field[lo + i : lo + i + count, 2 * pair + r].reshape(count * width, C))
            parts.append(jnp.concatenate(blocks, axis=1))
        return jnp.concatenate(parts, axis=0)

    def conv_forward(field, W, lo, count, taps=(0, 1, 2)):
        lhs = window(field, taps, lo, count)
        deep = len(taps) * 4 * C
        total = None
        for k in (1, 0, 2):
            rhs = W[k, taps[0] : taps[-1] + 1].reshape(deep, 2 * C)
            got = jnp.dot(lhs, rhs, preferred_element_type=F32)
            got = zero_shift(got, k - 1, width)
            total = got if total is None else total + got
        return total

    def conv_backward(field, V, lo, count, taps=(0, 1, 2)):
        lhs = window(field, [2 - i for i in taps], lo, count)
        total = None
        for k in (1, 0, 2):
            rhs = jnp.concatenate([V[k, i] for i in taps], axis=1)
            got = lax.dot_general(lhs, rhs, (((1,), (1,)), ((), ())), preferred_element_type=F32)
            got = zero_shift(got, 1 - k, width)
            total = got if total is None else total + got
        return total

    def put(dst, at_f, at_r, values):
        deep = values.shape[0] // pairs
        count = deep // width
        for pair in range(pairs):
            for o in range(2):
                part = values[pair * deep : (pair + 1) * deep, o * C : (o + 1) * C]
                dst[at_f : at_f + count, at_r + 2 * pair + o] = part.reshape(count, width, C).astype(dst.dtype)

    def get(src, at_f, at_r, count):
        parts = []
        for pair in range(pairs):
            blocks = [src[at_f : at_f + count, at_r + 2 * pair + o].reshape(count * width, C) for o in range(2)]
            parts.append(jnp.concatenate(blocks, axis=1))
        return jnp.concatenate(parts, axis=0).astype(F32)

    def first_conv(part):
        if part == 0:
            first_out = conv_forward(X, W1, 0, half, (0, 1)) + early[1]
        else:
            first_out = conv_forward(X, W1, half, half)
        sigma = sigmoid(first_out)
        put(H, 2 + part * half, 1, first_out * sigma)
        slope[part] = sigma * (1.0 + first_out * (1.0 - sigma))

    eye = (
        lax.broadcasted_iota(jnp.int32, (C, C), 0) == lax.broadcasted_iota(jnp.int32, (C, C), 1)
    ).astype(BF16)
    spots = [(i, j) for i in range(3) for j in range(3)]

    def turned(values):
        return lax.dot_general(eye, values, (((1,), (1,)), ((), ())), preferred_element_type=F32).astype(BF16)

    groups = ((0, 4), (4, 3))

    def place_of(pair):
        group = min(pair // 8, 1)
        base, size = groups[group]
        at = pair - 8 * group
        return at // size, base + at % size

    class Taps:
        def __init__(self, g):
            self.g, self.held, self.stored, self.sent = g, [], 0, 0

        def add(self, side):
            self.held.append(side)
            if len(self.held) == 2:
                part, slot = place_of(self.stored)
                a, b = self.held
                both = jnp.concatenate([a.reshape(nz, ny, oc, C), b.reshape(nz, ny, oc, C)], axis=2)
                if part == 1:
                    both = jnp.transpose(both, (1, 0, 2, 3))
                PP[self.g, part, :, :, slot] = both.astype(BF16)
                self.held = []
                self.stored += 1
                if self.stored in (8, 14):
                    pair_start(self.g, self.sent)
                    self.sent += 1

    def first_kernel_gradient():
        grads = G[0:FR, 1 : 1 + RT].reshape(cells, C).astype(F32)
        for k in range(3):
            LT[k * C : (k + 1) * C] = turned(zero_shift(grads, 1 - k, width).astype(BF16))
        taps = Taps(0)
        for m in range(5):
            pieces = spots[2 * m : 2 * m + 2]
            rhs = jnp.concatenate([X[i : i + FR, j : j + RT].reshape(cells, C) for i, j in pieces], axis=1)
            got = jnp.dot(LT[...], rhs, preferred_element_type=F32)
            for n in range(len(pieces)):
                for k in range(3):
                    taps.add(got[k * C : (k + 1) * C, n * C : (n + 1) * C])
        taps.add(jnp.zeros((C, C), F32))

    tall = (RT + 2) * width

    def turn_frame(f):
        CT[:, f * tall : (f + 1) * tall] = turned(C_[f].reshape(tall, C))
        CO[:, f * RT * width : (f + 1) * RT * width] = turned(C_[f, 1 : 1 + RT].reshape(RT * width, C))

    def second_kernel_gradient():
        hidden = H[2 : 2 + FR, 1 : 1 + RT].reshape(cells, C).astype(F32)
        rhs = jnp.concatenate([zero_shift(hidden, k - 1, width).astype(BF16) for k in range(3)], axis=1)

        def turned_window(a, b):
            if b == 1:
                return CO[:, a * RT * width : (a + FR) * RT * width]
            return jnp.concatenate(
                [CT[:, f * tall + b * width : f * tall + (b + RT) * width] for f in range(a, a + FR)], axis=1
            )

        taps = Taps(1)
        for i in range(3):
            lhs = jnp.concatenate([turned_window(2 - i, 2 - j) for j in range(3)], axis=0)
            got = jnp.dot(lhs, rhs, preferred_element_type=F32)
            for j in range(3):
                for k in range(3):
                    taps.add(got[j * C : (j + 1) * C, k * C : (k + 1) * C])
        taps.add(jnp.zeros((C, C), F32))

    swaps, axes = {}, {0: [], 1: []}

    def cut(ref, group):
        base, size = groups[group]
        return ref.at[:, :, base : base + size]

    def pair_start(g, group):
        copy = remote(
            cut(PP.at[g, 1 - core], group), cut(R0.at[g], group), s0.at[g, group], r0.at[g, group], (tm, partner)
        )
        swaps[g, group] = copy
        sent.append(copy)

    first, second = (1 - core) * z + core * y, (1 - core) * y + core * z

    def axis_peer(d, turn):
        along_z = (1 - core) * (1 - turn) + core * turn
        return (((z + d * along_z) % nz) * ny + (y + d * (1 - along_z)) % ny, rows)

    def axis_start(g):
        for group in range(len(groups)):
            swaps[g, group].wait_recv()
        for d in range(nz):
            at = (first + nz - d) % nz
            S1[g, at] = (PP[g, core, at].astype(F32) + R0[g, at].astype(F32)).astype(BF16)
            if d:
                copy = remote(S1.at[g, at], A1.at[g, d - 1], s1.at[g, d - 1], r1.at[g, d - 1], axis_peer(nz - d, 0))
                axes[g].append(copy)
                sent.append(copy)

    def axis_turn(g):
        for copy in axes[g]:
            copy.wait_recv()
        total = S1[g, first].astype(F32)
        for d in range(1, nz):
            total = total + A1[g, d - 1].astype(F32)
        S2[g] = total.astype(BF16)
        axes[g] = []
        for d in range(1, nz):
            at = (second + d) % nz
            copy = remote(S2.at[g, at], A2.at[g, d - 1], s3.at[g, d - 1], r3.at[g, d - 1], axis_peer(d, 1))
            axes[g].append(copy)
            sent.append(copy)

    last = []
    scale = 1.0 / math.sqrt(cells_all)

    def axes_finish(g):
        for copy in axes[g]:
            copy.wait_recv()
        total = S2[g, second].astype(F32)
        for d in range(1, nz):
            total = total + A2[g, d - 1].astype(F32)
        E[g, core, x] = total.astype(BF16)
        more = [
            remote(
                E.at[g, core, x], E.at[g, core, x], s2.at[g, o - 1], r2.at[g, o - 1], (tm, (rows + o) % nrows)
            )
            for o in range(1, nrows)
        ]
        last.extend(more)

    def give(g, out):
        for o in range(1, nrows):
            giver = (rows + nrows - o) % nrows
            block = E.at[g, giver % 2, giver // 2]
            pltpu.make_async_remote_copy(
                src_ref=block, dst_ref=block, send_sem=s2.at[g, o - 1], recv_sem=r2.at[g, o - 1],
                device_id=(tm, (rows + o) % nrows), device_id_type=MESH,
            ).wait_recv()
        for pair in range(14):
            part, slot = place_of(pair)
            values = E[g, part, 0, slot].astype(F32)
            for at in range(1, nx):
                values = values + E[g, part, at, slot].astype(F32)
            values = values * scale
            out[2 * pair] = values[0:oc]
            if pair < 13:
                out[2 * pair + 1] = values[oc : 2 * oc]

    receive_rows(rows_f, F, True)
    for f in range(2, 2 + FR):
        silu_into(f, slice(0, 1))
        silu_into(f, slice(RT + 1, RT + 2))
    arrived("W1")
    first_conv(1)
    time_h = send_time(2, H, 2, 1, H, True)
    arrived("C")
    receive_rows(rows_c, C_, False)
    arrived("V2")
    early[0] = conv_backward(C_, V2, 0, half)
    early[1] = conv_forward(X, W1, 0, half, (2,))
    early[2] = conv_backward(C_, V2, half, half, (2,))
    for f in range(FR):
        turn_frame(f)

    receive_time(time_f, F, True)
    for f in range(2):
        silu_into(f, slice(0, RT + 2))
    first_conv(0)
    rows_h = send_rows(2, H, 2, 1, H, True)
    put(G, 0, 1, early[0] * slope[0])
    time_g = send_time(3, G, 0, 1, G, False)

    receive_time(time_c, C_, False)
    for f in range(FR, FR + 2):
        turn_frame(f)
    second_kernel_gradient()
    put(G, half, 1, (conv_backward(C_, V2, half, half, (0, 1)) + early[2]) * slope[1])
    rows_g = send_rows(3, G, 0, 1, G, False)
    axis_start(1)
    first_kernel_gradient()
    axis_start(0)
    axis_turn(1)
    axis_turn(0)
    receive_rows(rows_h, H, True)
    receive_time(time_h, H, True)
    arrived("W2")
    put(out_b, 0, 0, get(F, 2, 1, FR) + conv_forward(H, W2, 0, FR))

    axes_finish(1)
    receive_rows(rows_g, G, False)
    receive_time(time_g, G, False)
    arrived("V1")
    feats = get(F, 2, 1, FR)
    sigma = sigmoid(feats)
    turn = sigma * (1.0 + feats * (1.0 - sigma))
    put(out_g, 0, 0, get(C_, 0, 1, FR) + conv_backward(G, V1, 0, FR) * turn)

    axes_finish(0)
    for copy in sent:
        copy.wait_send()
    give(1, out_2)
    give(0, out_1)
    for copy in last:
        copy.wait_send()


def hand_out(a, b, c, d, out_a, out_b, out_c, out_d, sems):
    pairs = ((a, out_a), (b, out_b), (c, out_c), (d, out_d))
    copies = [pltpu.make_async_copy(src, dst, sems.at[n]) for n, (src, dst) in enumerate(pairs)]
    for copy in copies:
        copy.start()
    for copy in copies:
        copy.wait()


def build(geom, features, cotangent, first_kernel, second_kernel):
    nz, ny, nx, width, cells_all = geom
    FR, RT = features.shape[0], features.shape[1]
    ntm = nz * ny
    oc = C // ntm
    tall = 2 * oc
    cells = FR * RT * width
    pad = pltpu.VMEM((FR + 2, RT + 2, width, C), BF16)
    forward = pltpu.VMEM((3, 3, 4, C, 2 * C), BF16)
    backward = pltpu.VMEM((3, 3, 2 * C, 4 * C), BF16)
    block = (7, tall, C)
    scratch = [
        pad, pad, pad, pad, pad,
        forward, backward, forward, backward,
        pltpu.VMEM((2, cells // 4, 2 * C), F32),
        pltpu.VMEM((3, cells // 4, 2 * C), F32),
        pltpu.VMEM((3 * C, cells), BF16),
        pltpu.VMEM((C, (FR + 2) * (RT + 2) * width), BF16),
        pltpu.VMEM((C, (FR + 2) * RT * width), BF16),
        pltpu.VMEM((2, 2, nz, ny) + block, BF16),
        pltpu.VMEM((2, nz, ny) + block, BF16),
        pltpu.VMEM((2, nz, ny) + block, BF16),
        pltpu.VMEM((2, ny) + block, BF16),
        pltpu.VMEM((2, nz - 1, ny) + block, BF16),
        pltpu.VMEM((2, nz - 1) + block, BF16),
        pltpu.VMEM((2, 2, nx) + block, BF16),
        pltpu.SemaphoreType.DMA((50,)),
        pltpu.SemaphoreType.DMA((4, 5)),
        pltpu.SemaphoreType.DMA((4, 5)),
        pltpu.SemaphoreType.DMA((2, 3)),
        pltpu.SemaphoreType.DMA((2, 3)),
        pltpu.SemaphoreType.DMA((2, nz - 1)),
        pltpu.SemaphoreType.DMA((2, nz - 1)),
        pltpu.SemaphoreType.DMA((2, 2 * nx - 1)),
        pltpu.SemaphoreType.DMA((2, 2 * nx - 1)),
        pltpu.SemaphoreType.DMA((2, nz - 1)),
        pltpu.SemaphoreType.DMA((2, nz - 1)),
    ]
    anywhere = pl.BlockSpec(memory_space=pl.ANY)
    features, cotangent, first_kernel, second_kernel = [
        pltpu.with_memory_space_constraint(value, pltpu.HBM)
        for value in (features, cotangent, first_kernel, second_kernel)
    ]
    field = jax.ShapeDtypeStruct(features.shape, BF16)
    grads = jax.ShapeDtypeStruct((27, oc, C), F32)
    block_out, grad_input, g1, g2 = pl.pallas_call(
        functools.partial(kernel, geom),
        out_shape=(field, field, grads, grads),
        in_specs=[anywhere] * 4,
        out_specs=(pl.BlockSpec(memory_space=pltpu.VMEM),) * 4,
        scratch_shapes=scratch,
        compiler_params=pltpu.CompilerParams(
            collective_id=0, has_side_effects=True, vmem_limit_bytes=48 * 1024 * 1024
        ),
    )(features, cotangent, first_kernel, second_kernel)

    block_out, grad_input, g1, g2 = pl.pallas_call(
        hand_out,
        out_shape=(field, field, grads, grads),
        in_specs=[anywhere] * 4,
        out_specs=(anywhere,) * 4,
        scratch_shapes=[pltpu.SemaphoreType.DMA((4,))],
        compiler_params=pltpu.CompilerParams(vmem_limit_bytes=8 * 1024 * 1024),
    )(block_out, grad_input, g1, g2)

    def place(values):
        return jnp.transpose(values.reshape(3, 3, 3, oc, C), (0, 1, 2, 4, 3))

    return block_out, grad_input, place(g1), place(g2)


def solution(mesh, sides=(4, 4, 4)):
    nz, ny, nx = sides

    def on_device(features, cotangent, first_kernel, second_kernel):
        width = features.shape[2]
        cells_all = features.shape[0] * features.shape[1] * width * nz * ny * nx * 2
        geom = (nz, ny, nx, width, cells_all)
        return build(geom, features, cotangent, first_kernel, second_kernel)

    return jax.shard_map(
        on_device,
        mesh=mesh,
        in_specs=(P("tm", "rows", None, None), P("tm", "rows", None, None), P(), P()),
        out_specs=(
            P("tm", "rows", None, None),
            P("tm", "rows", None, None),
            P(None, None, None, None, "tm"),
            P(None, None, None, None, "tm"),
        ),
        check_vma=False,
    )
```
